32 devices in a mesh: blk: 4 (over y, x), uly: 8 (over z, core).
Axes of the slice: x: 2, y: 2, z: 4, core: 2. Of those that a mesh axis runs over, the one named last changes fastest.
Arguments:
- hidden_in: bfloat16 [4096, 2048], P(('blk', 'uly')), may hold values from -18 to 18
- queries: bfloat16 [4096, 2048], P(('blk', 'uly')), may hold values from -41 to 41
- keys: bfloat16 [4096, 256], P(('blk', 'uly')), may hold values from -4 to 4
- values: bfloat16 [4096, 256], P(('blk', 'uly')), may hold values from -24 to 24
- segment_ids: int32 [4096], P(('blk', 'uly')), may hold values from 0 to 63, never falling along the last dimension, each value on 1 to 512 neighbouring positions
- prefix_ids: int32 [64], replicated, may hold values from 0 to 63
- o_weight: bfloat16 [2048, 2048], replicated, may hold values from -0.125 to 0.125
- post_gain: float32 [2048], replicated, may hold values from 0.1 to 1.9
- expert_ids: int32 [4096, 8], P(('blk', 'uly')), may hold values from 0 to 31, all different within a row; in each aligned block of 128 rows (0 to 127, 128 to 255, ...) at most 36 rows name the same one
- gates: float32 [4096, 8], P(('blk', 'uly')), may hold values from 0.05 to 1
- w_gate: bfloat16 [32, 2048, 768], P(('blk', 'uly')), may hold values from -0.125 to 0.125
- w_up: bfloat16 [32, 2048, 768], P(('blk', 'uly')), may hold values from -0.125 to 0.125
- w_down: bfloat16 [32, 768, 2048], P(('blk', 'uly')), may hold values from -0.21875 to 0.21875
Outputs:
- layer_out: bfloat16 [4096, 2048], P(('blk', 'uly'))
The draws below stay inside these ranges and needn't reach their ends.
Inputs may be any that keep to these rules, and one draw needn't show every extreme that they name: `segment_ids`: never falling along the window; each segment holds 1 to 512 positions, one exactly 512. `expert_ids`: each row names 8 different experts; within the rows of one device (aligned blocks of 128 tokens) no expert is named more than 36 times.
All inputs are finite; a program needn't handle non-finite values.
Results may differ from the reference program's by a relative error of at most 0.006.
Values may be sent and summed in bfloat16 or wider, within the bound.
No kernel may reach another device: no remote copies, remote signals or barrier semaphores. Data moves between devices by JAX's collectives and lax.ppermute only.
A program may use at most 128 MiB of HBM per device.

```python
import math
import jax
import jax.numpy as jnp
import numpy as np
from jax import lax

D = 2048
QUERY_HEADS = 16
KEY_VALUE_HEADS = 2
HEAD_SIZE = 128
FFE = 768
TOPK = 8
SEGS = 64
MOSTSEG = 512
TOK_DEV = 128
WINDOW_TOKENS = 4096
EXPERTS = 32
CAP = 36


def attention_inputs(key):
    base = jax.random.fold_in(key, 4242)
    key_q = jax.random.fold_in(base, 0)
    key_matrix = jax.random.fold_in(base, 1)
    key_strength = jax.random.fold_in(base, 3)
    key_offset = jax.random.truncated_normal(key_matrix, -4.0, 4.0, (WINDOW_TOKENS, KEY_VALUE_HEADS * HEAD_SIZE), jnp.float32)
    query_base = jax.random.truncated_normal(key_q, -4.0, 4.0, (WINDOW_TOKENS, QUERY_HEADS * HEAD_SIZE), jnp.float32)
    special = jnp.zeros((WINDOW_TOKENS,), bool)
    levels = jnp.array([8.0, 16.0, 24.0], jnp.float32)
    strength = levels[jax.random.randint(key_strength, (WINDOW_TOKENS,), 0, 3)]
    broadened_keys = jnp.repeat(key_offset.reshape(WINDOW_TOKENS, KEY_VALUE_HEADS, HEAD_SIZE), QUERY_HEADS // KEY_VALUE_HEADS, axis=1).reshape(WINDOW_TOKENS, QUERY_HEADS * HEAD_SIZE)
    query_full = jnp.where(special[:, None], strength[:, None] * broadened_keys, query_base)
    next_special = jnp.concatenate([special[1:], jnp.zeros((1,), bool)])
    next_strength = jnp.concatenate([strength[1:], strength[:1]])
    next_keys = jnp.concatenate([key_offset[1:], key_offset[:1]], axis=0)
    shrink = 2.0 / (next_strength * math.sqrt(HEAD_SIZE))
    key_full = jnp.where(next_special[:, None], (1.0 - shrink[:, None]) * next_keys, key_offset)
    return (query_full, key_full)


def draw_queries(key, part):
    return attention_inputs(key)[0].astype(jnp.bfloat16)


def draw_keys(key, part):
    return attention_inputs(key)[1].astype(jnp.bfloat16)


def draw_hidden_in(key, part):
    base = jax.random.fold_in(key, 1117)
    key_main, key_col = jax.random.split(base, 2)
    column_scale = jnp.exp(jax.random.uniform(key_col, (1, D), jnp.float32, -0.7, 0.7))
    noise = jax.random.truncated_normal(key_main, -4.0, 4.0, (WINDOW_TOKENS, D), jnp.float32)
    result = 0.5 * noise * column_scale
    return result.astype(jnp.bfloat16)


def with_ends(entries, rng, least, top_value):
    spot = [jax.random.randint(jax.random.fold_in(rng, axis), (), 0, length) for axis, length in enumerate(entries.shape)]
    main_axis = entries.shape.index(max(entries.shape))
    beside = spot[:main_axis] + [(spot[main_axis] + 1) % entries.shape[main_axis]] + spot[main_axis + 1:]
    return entries.at[tuple(spot)].set(least).at[tuple(beside)].set(top_value)


def block_scale(stream_key, dims, cuts, low, largest):
    def one(position, shards_of):
        draws = jax.random.uniform(jax.random.fold_in(jax.random.fold_in(stream_key, 6), position), (shards_of,), jnp.float32, low / len(cuts), largest / len(cuts))
        return jnp.repeat(jnp.exp(draws), dims[position] // shards_of).reshape((-1,) + (1,) * (len(dims) - position - 1))

    factor_of = one(*cuts[0])
    for cut in cuts[1:]:
        factor_of = factor_of * one(*cut)
    return factor_of


def split_up(number_of, total, most, lean):
    loads = [(1 << 20) // math.isqrt(rank ** lean) + 1 for rank in range(2, number_of + 1)]
    spare, counts = total - most - (number_of - 1), [1] * (number_of - 1)
    while spare > 0:
        free = [i for i in range(number_of - 1) if counts[i] < most]
        whole, budget = sum([loads[i] for i in free]), spare
        for i in free:
            extra = min(most - counts[i], max(1, budget * loads[i] // whole), spare)
            counts[i] = counts[i] + extra
            spare = spare - extra
    return np.array([most] + counts)


def uneven(own_key, count, total, reach, slope):
    if count == 2:
        one = jax.random.randint(own_key, (), max(1, total - reach), min(reach, total - 1) + 1)
        return jnp.stack([one, total - one])
    lengths = jnp.asarray(split_up(count, total, reach, slope), jnp.int32)
    twos = (count - 1) // 2
    giver, sink = lengths[1:1 + 2 * twos:2], lengths[2:2 + 2 * twos:2]
    room = jnp.minimum(giver - 1, reach - sink)
    moved = jax.random.randint(jax.random.fold_in(own_key, 1), (twos,), 0, 1 << 20) % (room + 1)
    lengths = lengths.at[1:1 + 2 * twos:2].set(giver - moved).at[2:2 + 2 * twos:2].set(sink + moved)
    return lengths[jax.random.permutation(jax.random.fold_in(own_key, 2), count)]


def shared_out(own_key, own, number, rows, number_of, top, most, lean):
    ranking = jax.random.permutation(own_key, number_of)
    crowded, usual = portions_of(number_of, rows * top, most, lean, True), portions_of(number_of, rows * top, most, lean, False)
    places = jnp.arange(number_of)

    def named(sizes, offset_by):
        used = int((sizes > 0).sum())
        fixed = max(1, used // 4)
        shifted = fixed + (places - fixed + offset_by * (used - fixed)) % max(1, number_of - fixed)
        return jnp.zeros((number_of,), jnp.int32).at[ranking[jnp.where(places < fixed, places, shifted)]].set(jnp.asarray(sizes, jnp.int32))

    sizes = jnp.where(number % 4 == 0, named(crowded, number // 4), named(usual, number - number // 4 - 1))
    mixed = jax.random.permutation(jax.random.fold_in(own, 3), number_of)
    giver, taker = mixed[0:number_of // 2 * 2:2], mixed[1:number_of // 2 * 2:2]
    margin = jnp.minimum(sizes[giver] - 1, most - sizes[taker]) // 2
    margin = jnp.where((giver == ranking[0]) | (taker == ranking[0]) | (sizes[taker] == 0), 0, jnp.maximum(margin, 0))
    shifted = jax.random.randint(jax.random.fold_in(own, 4), (number_of // 2,), 0, 1 << 20) % (margin + 1)
    sizes = sizes.at[giver].add(-shifted).at[taker].add(shifted)
    labels = jnp.searchsorted(jnp.cumsum(sizes), jnp.arange(rows * top), side="right").astype(jnp.int32)
    table = labels.reshape(top, rows).T
    table = table[jax.random.permutation(jax.random.fold_in(own, 1), rows)]
    offset_by = jax.random.randint(jax.random.fold_in(own, 2), (rows, 1), 0, top)
    return jnp.take_along_axis(table, (jnp.arange(top)[None, :] + offset_by) % top, axis=1)


def portions_of(count, total, bound, lean, full):
    loads = [(1 << 20) // math.isqrt(rank ** lean) + 1 for rank in range(1, count + 1)]
    largest = bound if full else min(bound, max(-(-total // count), total * loads[0] // sum(loads)))
    least = 1 if total - largest >= count - 1 else 0
    counts, surplus = [largest] + [least] * (count - 1), total - largest - least * (count - 1)
    while surplus > 0:
        movable = [i for i in range(1, count) if counts[i] < largest] or [i for i in range(1, count) if counts[i] < bound]
        pool, remaining = sum([loads[i] for i in movable]), surplus
        for i in movable:
            more = min(bound - counts[i], max(1, remaining * loads[i] // pool), surplus)
            counts[i] = counts[i] + more
            surplus = surplus - more
    return np.array(counts)


def centred(own_key, shape, deviation, bound, cuts=(), kind=jnp.bfloat16):
    values = deviation * jax.random.normal(own_key, shape, jnp.float32)
    if cuts:
        values = values * block_scale(own_key, shape, cuts, -0.22, 0.18)
    return jnp.clip(values, -bound, bound).astype(kind)


def setup_inputs(seed: int = 0) -> dict:
    key_of = jax.random.split(jax.random.key(seed), 14)
    hidden_in = draw_hidden_in(jax.random.fold_in(key_of[13], 71), 0)
    queries = draw_queries(jax.random.fold_in(key_of[13], 71), 0)
    keys = draw_keys(jax.random.fold_in(key_of[13], 71), 0)
    values = centred(key_of[3], (WINDOW_TOKENS, KEY_VALUE_HEADS * HEAD_SIZE), 4.0, 24.0, ((0, 32),))
    segment_ids = jnp.searchsorted(jnp.cumsum(uneven(key_of[4], SEGS, WINDOW_TOKENS, MOSTSEG, 1)), jnp.arange(WINDOW_TOKENS), side="right").astype(jnp.int32)
    prefix_ids = with_ends(jax.random.randint(key_of[5], (SEGS,), 0, SEGS), jax.random.fold_in(key_of[5], 1), 0, SEGS - 1).astype(jnp.int32)
    o_weight = centred(key_of[6], (QUERY_HEADS * HEAD_SIZE, D), (QUERY_HEADS * HEAD_SIZE) ** -0.5, 0.125)
    post_gain = jnp.clip(1.0 + 0.18 * jax.random.normal(key_of[7], (D,), jnp.float32), 0.1, 1.9)
    expert_ids_keys = jax.random.split(jax.random.fold_in(key_of[8], 1), WINDOW_TOKENS // TOK_DEV)
    expert_ids_turns = jax.random.permutation(jax.random.fold_in(key_of[8], 3), WINDOW_TOKENS // TOK_DEV)
    expert_ids = jax.vmap(lambda own, number: shared_out(jax.random.fold_in(key_of[8], 2), own, number, TOK_DEV, EXPERTS, TOPK, CAP, 1))(expert_ids_keys, expert_ids_turns).reshape((WINDOW_TOKENS, TOPK))
    gates = jnp.clip(jnp.exp(math.log(1.0) - 2.9957323 * jax.random.uniform(key_of[9], (WINDOW_TOKENS, TOPK), jnp.float32) ** block_scale(key_of[9], (WINDOW_TOKENS, TOPK), ((0, 32),), -0.2, 0.2)), 0.05, 1.0)
    w_gate = centred(key_of[10], (EXPERTS, D, FFE), D ** -0.5, 0.125, ((0, 32),))
    w_up = centred(key_of[11], (EXPERTS, D, FFE), D ** -0.5, 0.125, ((0, 32),))
    w_down = centred(key_of[12], (EXPERTS, FFE, D), FFE ** -0.5, 0.21875, ((0, 32),))
    return dict(hidden_in=hidden_in, queries=queries, keys=keys, values=values, segment_ids=segment_ids, prefix_ids=prefix_ids, o_weight=o_weight, post_gain=post_gain, expert_ids=expert_ids, gates=gates, w_gate=w_gate, w_up=w_up, w_down=w_down)


def reference(hidden_in, queries, keys, values, segment_ids, prefix_ids, o_weight, post_gain, expert_ids, gates, w_gate, w_up, w_down):
    group_width = QUERY_HEADS // KEY_VALUE_HEADS
    score_scale = 1.0 / math.sqrt(HEAD_SIZE)
    positions = jnp.arange(WINDOW_TOKENS, dtype=jnp.int32)
    query_prefix = prefix_ids[segment_ids]
    block_rows = min(512, WINDOW_TOKENS)
    block_count = WINDOW_TOKENS // block_rows

    def one_block(number):
        head_number = (number // block_count).astype(jnp.int32)
        row_start = (number % block_count * block_rows).astype(jnp.int32)
        query_block = lax.dynamic_slice(queries, (row_start, head_number * HEAD_SIZE), (block_rows, HEAD_SIZE))
        kv_head = head_number // group_width
        key_block = lax.dynamic_slice(keys, (jnp.int32(0), kv_head * HEAD_SIZE), (WINDOW_TOKENS, HEAD_SIZE))
        value_block = lax.dynamic_slice(values, (jnp.int32(0), kv_head * HEAD_SIZE), (WINDOW_TOKENS, HEAD_SIZE))
        scores = jnp.dot(query_block, key_block.T, preferred_element_type=jnp.float32) * score_scale
        query_pos = row_start + jnp.arange(block_rows, dtype=jnp.int32)
        query_seg = lax.dynamic_slice_in_dim(segment_ids, row_start, block_rows, 0)
        query_pre = lax.dynamic_slice_in_dim(query_prefix, row_start, block_rows, 0)
        visible = (positions[None, :] <= query_pos[:, None]) & ((segment_ids[None, :] == query_seg[:, None]) | (segment_ids[None, :] == query_pre[:, None]))
        row_top = lax.optimization_barrier(jnp.max(jnp.where(visible, scores, -1e+30), axis=1, keepdims=True))
        exp_scores = jnp.where(visible, jnp.exp(scores - row_top), 0.0)
        weight_sum = lax.optimization_barrier(jnp.sum(exp_scores, axis=1, keepdims=True))
        result = jnp.dot(exp_scores.astype(jnp.bfloat16), value_block, preferred_element_type=jnp.float32) / weight_sum
        return result.astype(jnp.bfloat16)
    pieces = lax.map(one_block, jnp.arange(QUERY_HEADS * block_count, dtype=jnp.int32))
    attended = pieces.reshape(QUERY_HEADS, WINDOW_TOKENS, HEAD_SIZE).transpose(1, 0, 2).reshape(WINDOW_TOKENS, QUERY_HEADS * HEAD_SIZE)
    mixed = hidden_in.astype(jnp.float32) + jnp.dot(attended, o_weight, preferred_element_type=jnp.float32)
    normed = (mixed * lax.rsqrt(lax.optimization_barrier(jnp.mean(mixed * mixed, axis=1, keepdims=True)) + 1e-06) * post_gain.astype(jnp.float32)).astype(jnp.bfloat16)
    share = gates / lax.optimization_barrier(jnp.sum(gates, axis=1, keepdims=True))
    flat_experts = expert_ids.reshape(-1)
    flat_share = share.reshape(-1)
    most_rows = EXPERTS * CAP

    def per_expert(running, expert):
        matches = flat_experts == expert
        found = jnp.nonzero(matches, size=most_rows, fill_value=0)[0].astype(jnp.int32)
        found_count = jnp.sum(matches.astype(jnp.int32))
        valid = jnp.arange(most_rows, dtype=jnp.int32) < found_count
        token_index = (found // TOPK).astype(jnp.int32)
        chosen_rows = normed[token_index]
        gate_proj = jnp.dot(chosen_rows, w_gate[expert], preferred_element_type=jnp.float32)
        up_proj = jnp.dot(chosen_rows, w_up[expert], preferred_element_type=jnp.float32)
        hidden_act = (jax.nn.silu(gate_proj) * up_proj).astype(jnp.bfloat16)
        expert_answer = jnp.dot(hidden_act, w_down[expert], preferred_element_type=jnp.float32).astype(jnp.bfloat16)
        row_weight = jnp.where(valid, flat_share[found], 0.0)
        running = running.at[token_index].add(expert_answer.astype(jnp.float32) * row_weight[:, None])
        return (running, None)
    routed, _ = lax.scan(per_expert, jnp.zeros((WINDOW_TOKENS, D), jnp.float32), jnp.arange(EXPERTS, dtype=jnp.int32))
    return (mixed + routed).astype(jnp.bfloat16)
```

```python
import functools
import math

import jax
import jax.numpy as jnp
from jax import lax
from jax.experimental import pallas as pl
from jax.experimental.pallas import tpu as pltpu
from jax.sharding import PartitionSpec as P

HEAD_SIZE = 128
EXTRA_ROWS = 8
FLOOR = -1e20
HIDDEN = -1e30


def chip_ring(count):
    return list(range(0, 1)) + list(range(1, count, 2)) + list(range(2, count, 2))[::-1]


def attend_kernel(first, last, counts, info_ref, q_ref, seg_q_ref, pre_q_ref, seg_k_ref, *refs):
    kv_refs, refs = refs[: len(counts)], refs[len(counts) :]
    if not first:
        top_in, sum_in, acc_in, *refs = refs
    if last:
        out_ref, top_ref, sum_ref, acc_ref = refs
    else:
        top_ref, sum_ref, acc_ref = refs
    kv_count, _, columns = q_ref.shape
    rows = seg_q_ref.shape[1]
    tiles = sum(counts)
    scale = math.log2(math.e) / math.sqrt(HEAD_SIZE)
    width = 2 * rows if columns % (2 * rows) == 0 else rows
    if first:
        top_ref[...] = jnp.full_like(top_ref, FLOOR)
        sum_ref[...] = jnp.zeros_like(sum_ref)
        acc_ref[...] = jnp.zeros_like(acc_ref)
    else:
        top_ref[...] = top_in[...]
        sum_ref[...] = sum_in[...]
        acc_ref[...] = acc_in[...]
    query_pos = info_ref[2 * tiles] + lax.broadcasted_iota(jnp.int32, (rows, rows), 1)
    start = 0
    for kv_ref, count in zip(kv_refs, counts, strict=True):

        def tile_step(i, _, kv_ref=kv_ref, start=start):
            tile = start + i

            @pl.when(info_ref[tile] > 0)
            def _():
                key_pos = info_ref[tiles + tile] + lax.broadcasted_iota(
                    jnp.int32, (rows, rows), 0
                )
                key_seg = jnp.broadcast_to(seg_k_ref[tile], (rows, rows)).T
                visible = (key_pos <= query_pos) & (
                    (key_seg == seg_q_ref[...]) | (key_seg == pre_q_ref[...])
                )
                bias = jnp.where(visible, 0.0, HIDDEN)
                bias = jnp.concatenate([bias] * (width // rows), axis=1)
                for g in range(kv_count):
                    key_tile = kv_ref[i, :rows, g * HEAD_SIZE : (g + 1) * HEAD_SIZE]
                    value_tile = kv_ref[
                        i, :rows, (kv_count + g) * HEAD_SIZE : (kv_count + g + 1) * HEAD_SIZE
                    ]
                    for at in range(0, columns, width):
                        part = pl.ds(at, width)
                        scores = (
                            jnp.dot(
                                key_tile, q_ref[g, :, part], preferred_element_type=jnp.float32
                            )
                            * scale
                            + bias
                        )
                        old_top = top_ref[g, :, part]
                        new_top = jnp.maximum(old_top, jnp.max(scores, axis=0, keepdims=True))
                        weights = jnp.exp2(scores - new_top)
                        rescale = jnp.exp2(old_top - new_top)
                        top_ref[g, :, part] = new_top
                        sum_ref[g, :, part] = sum_ref[g, :, part] * rescale + jnp.sum(
                            weights, axis=0, keepdims=True
                        )
                        acc_ref[g, :, part] = acc_ref[g, :, part] * rescale + jnp.dot(
                            value_tile,
                            weights.astype(jnp.bfloat16),
                            preferred_element_type=jnp.float32,
                        )

            return 0

        lax.fori_loop(0, count, tile_step, 0)
        start += count
    if last:
        for g in range(kv_count):
            for h in range(columns // rows):
                part = pl.ds(h * rows, rows)
                result = acc_ref[g, :, part] / sum_ref[g, :, part]
                at = (g * (columns // rows) + h) * HEAD_SIZE
                out_ref[:, at : at + HEAD_SIZE] = result.T.astype(out_ref.dtype)


def attend(kv_list, info, q_side, seg_q, pre_q, seg_k, state, last):
    kv_count, head, columns = q_side.shape
    rows = seg_q.shape[1]
    counts = tuple(kv.shape[0] for kv in kv_list)
    first = state is None
    state_shapes = [
        jax.ShapeDtypeStruct((kv_count, 1, columns), jnp.float32),
        jax.ShapeDtypeStruct((kv_count, 1, columns), jnp.float32),
        jax.ShapeDtypeStruct((kv_count, head, columns), jnp.float32),
    ]
    if last:
        out_shape = jax.ShapeDtypeStruct((rows, kv_count * columns // rows * head), jnp.bfloat16)
        scratch = [pltpu.VMEM(s.shape, s.dtype) for s in state_shapes]
    else:
        out_shape, scratch = state_shapes, []
    vmem = pl.BlockSpec(memory_space=pltpu.VMEM)
    operands = [q_side, seg_q, pre_q, seg_k, *kv_list, *(() if first else state)]
    return pl.pallas_call(
        functools.partial(attend_kernel, first, last, counts),
        out_shape=out_shape,
        in_specs=[pl.BlockSpec(memory_space=pltpu.SMEM)] + [vmem] * len(operands),
        out_specs=vmem if last else [vmem] * 3,
        scratch_shapes=scratch,
        compiler_params=pltpu.CompilerParams(vmem_limit_bytes=40 * 1024 * 1024),
        cost_estimate=pl.CostEstimate(
            flops=4 * len(kv_list) * rows * columns * kv_count * head,
            bytes_accessed=4_000_000,
            transcendentals=rows * columns * kv_count,
        ),
        name="attend_last" if last else "attend_own",
    )(info, *operands)


def shards(
    hidden_in,
    queries,
    keys,
    values,
    segment_ids,
    prefix_ids,
    o_weight,
    post_gain,
    expert_ids,
    gates,
    w_gate,
    w_up,
    w_down,
):
    bf16, f32 = jnp.bfloat16, jnp.float32
    tok, model_width = hidden_in.shape
    n_blk, n_uly = lax.axis_size("blk"), lax.axis_size("uly")
    chips = n_uly // 2
    experts_all = n_blk * n_uly
    top_count = expert_ids.shape[1]
    heads_all = queries.shape[1] // HEAD_SIZE
    kv_count = keys.shape[1] // HEAD_SIZE
    group = heads_all // kv_count
    blk, uly = lax.axis_index("blk"), lax.axis_index("uly")
    core, chip = uly % 2, uly // 2
    me = blk * n_uly + uly

    order = chip_ring(chips)
    ring_pairs = [
        (2 * order[i] + c, 2 * order[(i + 1) % chips] + c) for i in range(chips) for c in range(2)
    ]
    swap_pairs = [(u, u ^ 1) for u in range(n_uly)]
    next_chip = functools.partial(lax.ppermute, axis_name="uly", perm=ring_pairs)
    other_core = functools.partial(lax.ppermute, axis_name="uly", perm=swap_pairs)

    def other_block(x, m):
        return lax.ppermute(x, "blk", [(b, b ^ m) for b in range(n_blk)])

    order_of = jnp.array(order, jnp.int32)
    place_of = jnp.array([order.index(z) for z in range(chips)], jnp.int32)
    place = place_of[chip]
    chip_at = [order_of[(place - k) % chips] for k in range(chips)]

    share = gates / jnp.sum(gates, axis=1, keepdims=True)
    share_t, ids_t = share.T, expert_ids.T
    share_hi = share_t.astype(bf16)
    share_lo = (share_t - share_hi.astype(f32)).astype(bf16)
    kv_width = 2 * kv_count * HEAD_SIZE
    small = jnp.concatenate(
        [
            ids_t.astype(bf16).reshape(-1),
            share_hi.reshape(-1),
            share_lo.reshape(-1),
            segment_ids.astype(bf16),
        ]
    )
    small = jnp.pad(small, (0, EXTRA_ROWS * kv_width - small.shape[0]))
    values_t = values.reshape(tok, kv_count, HEAD_SIZE).transpose(2, 1, 0)
    kv_own = jnp.concatenate([keys, values_t.reshape(HEAD_SIZE, kv_count * tok)], axis=1)
    message = jnp.concatenate([kv_own, small.reshape(EXTRA_ROWS, kv_width)], axis=0)

    steps = [message]
    for _ in range(chips - 1):
        steps.append(next_chip(steps[-1]))
    kv_mine = jnp.stack(steps)
    kv_near = other_core(kv_mine)
    kv_far = [other_block(kv_mine, m) for m in range(1, n_blk)]
    kv_far_near = [other_core(kv) for kv in kv_far]

    def smalls(kv):
        return kv[:, tok:, :].reshape(kv.shape[0], -1)

    small_mine, small_near = smalls(kv_mine), smalls(kv_near)
    seg_at = 3 * top_count * tok

    seg_q = segment_ids
    table = jnp.arange(prefix_ids.shape[0], dtype=jnp.int32)
    pre_q = jnp.sum(jnp.where(seg_q[:, None] == table[None, :], prefix_ids[None, :], 0), axis=1)
    q_side = (
        queries.reshape(tok, kv_count, group, HEAD_SIZE)
        .transpose(1, 3, 2, 0)
        .reshape(kv_count, HEAD_SIZE, group * tok)
    )

    def tile_info(segs, devices):
        segs = segs.astype(jnp.int32)
        low, high = segs[:, 0], segs[:, -1]
        own = (low <= seg_q[-1]) & (high >= seg_q[0])
        shared = jnp.any(
            (pre_q[None, :] >= low[:, None]) & (pre_q[None, :] <= high[:, None]), axis=1
        )
        needed = (devices <= me) & (own | shared)
        return jnp.concatenate([needed.astype(jnp.int32), devices * tok, me[None] * tok])

    seg_row = seg_q.astype(f32)[None, :]
    pre_row = pre_q.astype(f32)[None, :]

    def device_list(sources):
        return jnp.stack(
            [b * n_uly + 2 * chip_at[k] + c for b, c in sources for k in range(chips)]
        ).astype(jnp.int32)

    segs_own = jnp.concatenate([small_mine[:, seg_at:][:, :tok], small_near[:, seg_at:][:, :tok]])
    state = attend(
        [kv_mine, kv_near],
        tile_info(segs_own, device_list([(blk, core), (blk, 1 - core)])),
        q_side,
        seg_row,
        pre_row,
        segs_own.astype(f32)[:, None, :],
        None,
        False,
    )
    segs_far = jnp.concatenate(
        [smalls(kv)[:, seg_at:][:, :tok] for kv in kv_far + kv_far_near]
    )
    far_sources = [(blk ^ m, core) for m in range(1, n_blk)] + [
        (blk ^ m, 1 - core) for m in range(1, n_blk)
    ]
    attended = attend(
        kv_far + kv_far_near,
        tile_info(segs_far, device_list(far_sources)),
        q_side,
        seg_row,
        pre_row,
        segs_far.astype(f32)[:, None, :],
        state,
        True,
    )

    mixed = hidden_in.astype(f32) + jnp.dot(attended, o_weight, preferred_element_type=f32)
    normed = (
        mixed * lax.rsqrt(jnp.mean(mixed * mixed, axis=1, keepdims=True) + 1e-06) * post_gain
    ).astype(bf16)

    capacity = max(2, 9 * tok * top_count // (8 * experts_all))
    count = top_count * tok
    expert_of = jnp.stack([(blk ^ m) * n_uly + uly for m in range(n_blk)]).astype(f32)

    def slots(small_rows):
        ids = small_rows[:, :count].reshape(chips, 1, top_count, tok).astype(f32)
        hi = small_rows[:, count : 2 * count].reshape(chips, 1, top_count, tok).astype(f32)
        lo = small_rows[:, 2 * count : 3 * count].reshape(chips, 1, top_count, tok).astype(f32)
        named = ids == expert_of[None, :, None, None]
        hit = jnp.any(named, axis=2)
        hi = jnp.sum(jnp.where(named, hi, 0.0), axis=2)
        lo = jnp.sum(jnp.where(named, lo, 0.0), axis=2)
        before = jnp.triu(jnp.ones((tok, tok), bf16), 1)
        rank = jnp.dot(
            hit.astype(bf16).reshape(chips * n_blk, tok), before, preferred_element_type=f32
        ).reshape(chips, n_blk, tok)
        return jnp.where(hit, rank, -1e6), hi, lo

    rank_a, hi_a, lo_a = slots(small_mine)
    rank_b, hi_b, lo_b = slots(small_near)
    rank = jnp.concatenate([rank_a, rank_b + capacity], axis=2).astype(jnp.int32)
    share_hi = jnp.concatenate([hi_a, hi_b], axis=2)
    share_lo = jnp.concatenate([lo_a, lo_b], axis=2)
    pair_rows = 2 * capacity
    slot_axis = jnp.arange(pair_rows, dtype=jnp.int32)
    chosen = rank[:, :, None, :] == slot_axis[None, None, :, None]

    rows_now = normed
    chunk_rows = []
    for k in range(chips):
        chunk_rows.append(rows_now)
        if k < chips - 1:
            rows_now = next_chip(rows_now)
    answers = []
    for k in range(chips):
        pair = jnp.concatenate([chunk_rows[k], other_core(chunk_rows[k])], axis=0)
        inbox = []
        for m in range(n_blk):
            picked = jnp.dot(
                chosen[k, m].astype(bf16), pair, preferred_element_type=f32
            ).astype(bf16)
            inbox.append(other_block(picked, m) if m else picked)
        rows = jnp.concatenate(inbox, axis=0)
        gate_proj = jnp.dot(rows, w_gate[0], preferred_element_type=f32)
        up_proj = jnp.dot(rows, w_up[0], preferred_element_type=f32)
        hidden_act = (jax.nn.silu(gate_proj) * up_proj).astype(bf16)
        answer = jnp.dot(hidden_act, w_down[0], preferred_element_type=f32).astype(bf16)
        answers.append(answer)

    partial = [None] * chips
    for k in [*range(1, chips), 0]:
        parts = [answers[k][m * pair_rows : (m + 1) * pair_rows] for m in range(n_blk)]
        back = jnp.concatenate([other_block(p, m) if m else p for m, p in enumerate(parts)], axis=0)
        spread = jnp.concatenate(
            [
                jnp.where(chosen[k], share[k][:, None, :], 0.0)
                .astype(bf16)
                .reshape(n_blk * pair_rows, 2 * tok)
                for share in (share_hi, share_lo)
            ],
            axis=0,
        )
        sums = lax.dot_general(
            spread,
            jnp.concatenate([back, back], axis=0),
            (((0,), (0,)), ((), ())),
            preferred_element_type=f32,
        )
        partial[k] = sums[:tok] + other_core(sums[tok:].astype(bf16)).astype(f32)
    total = None
    for k in range(1, chips):
        now = partial[k] if total is None else total.astype(f32) + partial[k]
        total = next_chip(now.astype(bf16))
    routed = partial[0] if total is None else partial[0] + total.astype(f32)
    return (mixed + routed).astype(bf16)


def solution(mesh):
    rows = P(("blk", "uly"), None)
    in_specs = (
        rows,
        rows,
        rows,
        rows,
        P(("blk", "uly")),
        P(),
        P(),
        P(),
        rows,
        rows,
        P(("blk", "uly"), None, None),
        P(("blk", "uly"), None, None),
        P(("blk", "uly"), None, None),
    )
    return jax.shard_map(shards, mesh=mesh, in_specs=in_specs, out_specs=rows, check_vma=False)
```

```python
import functools
import math

import jax
import jax.numpy as jnp
from jax import lax
from jax.experimental import pallas as pl
from jax.experimental.pallas import tpu as pltpu
from jax.sharding import PartitionSpec as P

HEAD_SIZE = 128
FLOOR = -1e20
HIDDEN = -1e30
BF16, F32 = jnp.bfloat16, jnp.float32


def chip_ring(count):
    return list(range(0, 1)) + list(range(1, count, 2)) + list(range(2, count, 2))[::-1]


def call(kernel, name, out_shape, operands, scalars=(), scratch=(), unused=(), cost=None):
    vmem = pl.BlockSpec(memory_space=pltpu.VMEM)
    several = isinstance(out_shape, (list, tuple))
    flops, moved, exps = cost or (0, 0, 0)
    return pl.pallas_call(
        kernel,
        out_shape=out_shape,
        in_specs=[pl.BlockSpec(memory_space=pltpu.SMEM)] * len(scalars)
        + [vmem] * len(operands)
        + [pl.BlockSpec(memory_space=pl.ANY)] * len(unused),
        out_specs=[vmem] * len(out_shape) if several else vmem,
        scratch_shapes=list(scratch),
        compiler_params=pltpu.CompilerParams(vmem_limit_bytes=48 * 1024 * 1024),
        cost_estimate=pl.CostEstimate(flops=flops, bytes_accessed=moved, transcendentals=exps),
        name=name,
    )(*scalars, *operands, *unused)


def message_kernel(core_ref, key_ref, value_ref, ids_ref, gates_ref, seg_ref, keep, give, small):
    first = core_ref[0] == 0
    k0, k1 = (key_ref[:, i * HEAD_SIZE : (i + 1) * HEAD_SIZE] for i in range(2))
    v0, v1 = (
        value_ref[:, i * HEAD_SIZE : (i + 1) * HEAD_SIZE].astype(F32).T.astype(BF16)
        for i in range(2)
    )
    keep[:, :HEAD_SIZE] = jnp.where(first, k0, k1)
    keep[:, HEAD_SIZE:] = jnp.where(first, v0, v1)
    give[:, :HEAD_SIZE] = jnp.where(first, k1, k0)
    give[:, HEAD_SIZE:] = jnp.where(first, v1, v0)
    share = gates_ref[...] / jnp.sum(gates_ref[...], axis=0, keepdims=True)
    share_hi = share.astype(BF16).astype(F32)
    segs = jnp.broadcast_to(seg_ref[...].astype(F32), share.shape)
    small[...] = jnp.concatenate(
        [ids_ref[...].astype(F32), share_hi, share - share_hi, segs], axis=0
    ).astype(BF16)


def turn_kernel(core_ref, query_ref, keep, give):
    first = core_ref[0] == 0
    half = keep.shape[1]
    tok = query_ref.shape[0]
    for h in range(half // tok):
        a, b = (
            query_ref[:, g * (half // tok) * HEAD_SIZE + h * HEAD_SIZE :][:, :HEAD_SIZE]
            .astype(F32)
            .T.astype(BF16)
            for g in range(2)
        )
        keep[:, h * tok : (h + 1) * tok] = jnp.where(first, a, b)
        give[:, h * tok : (h + 1) * tok] = jnp.where(first, b, a)


def attend_kernel(pieces, first, last, info_ref, q_own, q_near, seg_q_ref, pre_q_ref, *refs):
    seg_k_ref, refs = refs[0], refs[1:]
    kv_refs, refs = refs[:pieces], refs[pieces:]
    if not first:
        top_in, sum_in, acc_in, *refs = refs
    if last:
        own_ref, near_ref, top_ref, sum_ref, acc_ref, q_ref = refs
    else:
        top_ref, sum_ref, acc_ref, q_ref = refs
    columns, rows = q_own.shape[1], seg_q_ref.shape[2]
    tiles = 2 * pieces
    scale = math.log2(math.e) / math.sqrt(HEAD_SIZE)
    width = 2 * rows
    q_ref[0] = q_own[...]
    q_ref[1] = q_near[...]
    if first:
        top_ref[...] = jnp.full_like(top_ref, FLOOR)
        sum_ref[...] = jnp.zeros_like(sum_ref)
        acc_ref[...] = jnp.zeros_like(acc_ref)
    else:
        top_ref[...] = top_in[...]
        sum_ref[...] = sum_in[...]
        acc_ref[...] = acc_in[...]
    for piece, kv_ref in enumerate(kv_refs):

        def step(i, _, piece=piece, kv_ref=kv_ref):
            j, g = i // 2, i % 2
            tile = 2 * piece + j

            @pl.when(info_ref[g * tiles + tile] > 0)
            def _():
                square = (rows, rows)
                key_pos = info_ref[2 * tiles + tile] + lax.broadcasted_iota(jnp.int32, square, 0)
                query_pos = info_ref[3 * tiles + g] + lax.broadcasted_iota(jnp.int32, square, 1)
                key_seg = jnp.broadcast_to(seg_k_ref[tile], square).T
                visible = (key_pos <= query_pos) & (
                    (key_seg == seg_q_ref[g]) | (key_seg == pre_q_ref[g])
                )
                bias = jnp.where(visible, 0.0, HIDDEN)
                bias = jnp.concatenate([bias] * (width // rows), axis=1)
                key_tile = kv_ref[j, :, :HEAD_SIZE]
                value_tile = kv_ref[j, :, HEAD_SIZE:]
                for at in range(0, columns, width):
                    part = pl.ds(at, width)
                    scores = (
                        jnp.dot(key_tile, q_ref[g, :, part], preferred_element_type=F32) * scale
                        + bias
                    )
                    old_top = top_ref[g, :, part]
                    new_top = jnp.maximum(old_top, jnp.max(scores, axis=0, keepdims=True))
                    weights = jnp.exp2(scores - new_top)
                    rescale = jnp.exp2(old_top - new_top)
                    top_ref[g, :, part] = new_top
                    sum_ref[g, :, part] = sum_ref[g, :, part] * rescale + jnp.sum(
                        weights, axis=0, keepdims=True
                    )
                    acc_ref[g, :, part] = acc_ref[g, :, part] * rescale + jnp.dot(
                        value_tile, weights.astype(BF16), preferred_element_type=F32
                    )

            return 0

        lax.fori_loop(0, 4, step, 0)
    if last:
        for g, out_ref in enumerate((own_ref, near_ref)):
            for h in range(columns // rows):
                part = pl.ds(h * rows, rows)
                result = acc_ref[g, :, part] / sum_ref[g, :, part]
                out_ref[:, h * HEAD_SIZE : (h + 1) * HEAD_SIZE] = result.T.astype(BF16)


def attend(kv_list, info, q_own, q_near, seg_q, pre_q, seg_k, state, last):
    head, columns = q_own.shape
    rows = seg_q.shape[2]
    first = state is None
    state_shapes = [
        jax.ShapeDtypeStruct((2, 1, columns), F32),
        jax.ShapeDtypeStruct((2, 1, columns), F32),
        jax.ShapeDtypeStruct((2, head, columns), F32),
    ]
    scratch = [pltpu.VMEM((2, head, columns), BF16)]
    if last:
        out_shape = [jax.ShapeDtypeStruct((rows, columns // rows * head), BF16)] * 2
        scratch = [pltpu.VMEM(s.shape, s.dtype) for s in state_shapes] + scratch
    else:
        out_shape = state_shapes
    return call(
        functools.partial(attend_kernel, len(kv_list), first, last),
        "attend_last" if last else "attend_own",
        out_shape,
        [q_own, q_near, seg_q, pre_q, seg_k, *kv_list, *(() if first else state)],
        scalars=[info],
        scratch=scratch,
        cost=(2_000_000_000, 4_000_000, 1_000_000),
    )


def project_kernel(core_ref, own_ref, got_ref, weight_ref, hidden_ref, gain_ref, mixed_ref, out_ref):
    core = core_ref[0]
    half = own_ref.shape[1]
    width = hidden_ref.shape[1]
    block = math.gcd(width, 512)
    own_at = pl.multiple_of(core * half, half)
    got_at = pl.multiple_of((1 - core) * half, half)

    def step(i, total):
        part = pl.ds(pl.multiple_of(i * block, block), block)
        now = (
            hidden_ref[:, part].astype(F32)
            + jnp.dot(
                own_ref[...], weight_ref[pl.ds(own_at, half), part], preferred_element_type=F32
            )
            + jnp.dot(
                got_ref[...], weight_ref[pl.ds(got_at, half), part], preferred_element_type=F32
            )
        )
        mixed_ref[:, part] = now
        return total + jnp.sum(now * now, axis=1, keepdims=True)

    total = lax.fori_loop(0, width // block, step, jnp.zeros((own_ref.shape[0], 1), F32))
    factor = lax.rsqrt(total / width + 1e-06)
    out_ref[...] = (mixed_ref[...] * factor * gain_ref[...]).astype(BF16)


def pick_kernel(n_blk, own_ref, near_ref, rank_ref, *outs):
    tok, width = own_ref.shape
    slots = outs[0].shape[0]
    block = math.gcd(width, 512)
    slot = lax.broadcasted_iota(jnp.int32, (slots, 2 * tok), 0)
    chosen = jnp.concatenate(
        [jnp.where(rank_ref[m] == slot, 1.0, 0.0) for m in range(n_blk)], axis=0
    ).astype(BF16)

    def step(i, _):
        part = pl.ds(pl.multiple_of(i * block, block), block)
        pair = jnp.concatenate([own_ref[:, part], near_ref[:, part]], axis=0)
        rows = jnp.dot(chosen, pair, preferred_element_type=F32)
        for m in range(n_blk):
            outs[m][:, part] = rows[m * slots : (m + 1) * slots].astype(BF16)
        return 0

    lax.fori_loop(0, width // block, step, 0)


def expert_kernel(n_blk, *refs):
    ins, (gate_ref, up_ref, down_ref), refs = refs[:n_blk], refs[n_blk : n_blk + 3], refs[n_blk + 3 :]
    outs, (rows_ref, act_ref) = refs[-n_blk - 2 : -2], refs[-2:]
    slots, width = ins[0].shape
    inner = gate_ref.shape[1]
    rows_ref[...] = jnp.concatenate([r[...].astype(F32) for r in ins], axis=0).astype(BF16)
    block = math.gcd(inner, 256)

    def hidden(i, _):
        part = pl.ds(pl.multiple_of(i * block, block), block)
        gate = jnp.dot(rows_ref[...], gate_ref[:, part], preferred_element_type=F32)
        up = jnp.dot(rows_ref[...], up_ref[:, part], preferred_element_type=F32)
        act_ref[:, part] = (gate / (1.0 + jnp.exp(-gate)) * up).astype(BF16)
        return 0

    lax.fori_loop(0, inner // block, hidden, 0)
    wide = math.gcd(width, 512)

    def answer(i, _):
        part = pl.ds(pl.multiple_of(i * wide, wide), wide)
        rows = jnp.dot(act_ref[...], down_ref[:, part], preferred_element_type=F32)
        for m in range(n_blk):
            outs[m][:, part] = rows[m * slots : (m + 1) * slots].astype(BF16)
        return 0

    lax.fori_loop(0, width // wide, answer, 0)


def spread_kernel(n_blk, *refs):
    backs, (place_ref, own_ref, near_ref) = refs[:n_blk], refs[n_blk : n_blk + 3]
    slots, width = backs[0].shape
    tok = own_ref.shape[0]
    place = place_ref[...]
    lane = lax.broadcasted_iota(jnp.int32, (2 * tok, n_blk * slots), 1).astype(F32)
    weight_hi = jnp.zeros(lane.shape, F32)
    weight_lo = jnp.zeros(lane.shape, F32)
    for m in range(n_blk):
        hit = lane == place[:, m : m + 1]
        weight_hi = weight_hi + jnp.where(hit, place[:, n_blk + m : n_blk + m + 1], 0.0)
        weight_lo = weight_lo + jnp.where(hit, place[:, 2 * n_blk + m : 2 * n_blk + m + 1], 0.0)
    weight_hi, weight_lo = weight_hi.astype(BF16), weight_lo.astype(BF16)
    block = math.gcd(width, 512)

    def step(i, _):
        part = pl.ds(pl.multiple_of(i * block, block), block)
        rows = jnp.concatenate([r[:, part].astype(F32) for r in backs], axis=0).astype(BF16)
        sums = jnp.dot(weight_hi, rows, preferred_element_type=F32) + jnp.dot(
            weight_lo, rows, preferred_element_type=F32
        )
        own_ref[:, part] = sums[:tok]
        near_ref[:, part] = sums[tok:].astype(BF16)
        return 0

    lax.fori_loop(0, width // block, step, 0)


def shards(
    hidden_in,
    queries,
    keys,
    values,
    segment_ids,
    prefix_ids,
    o_weight,
    post_gain,
    expert_ids,
    gates,
    w_gate,
    w_up,
    w_down,
):
    tok, model_width = hidden_in.shape
    n_blk, n_uly = lax.axis_size("blk"), lax.axis_size("uly")
    chips = n_uly // 2
    experts_all = n_blk * n_uly
    top_count = expert_ids.shape[1]
    columns = queries.shape[1] // HEAD_SIZE // 2 * tok
    blk, uly = lax.axis_index("blk"), lax.axis_index("uly")
    core, chip = uly % 2, uly // 2
    me = blk * n_uly + uly
    core_here = core.astype(jnp.int32)[None]

    order = chip_ring(chips)
    ring_pairs = [
        (2 * order[i] + c, 2 * order[(i + 1) % chips] + c) for i in range(chips) for c in range(2)
    ]
    swap_pairs = [(u, u ^ 1) for u in range(n_uly)]
    next_chip = functools.partial(lax.ppermute, axis_name="uly", perm=ring_pairs)
    other_core = functools.partial(lax.ppermute, axis_name="uly", perm=swap_pairs)

    def other_block(x, m):
        return lax.ppermute(x, "blk", [(b, b ^ m) for b in range(n_blk)])

    def shape(*dims, dtype=BF16):
        return jax.ShapeDtypeStruct(dims, dtype)

    keep, give, small = call(
        message_kernel,
        "message",
        [shape(tok, 2 * HEAD_SIZE), shape(tok, 2 * HEAD_SIZE), shape(4 * top_count, tok)],
        [keys, values, expert_ids.T, gates.T, segment_ids[None, :]],
        scalars=[core_here],
    )
    small_chip = jnp.stack([small, other_core(small)])
    kv_chip = jnp.stack([keep, other_core(give)])
    small_steps, kv_steps = [small_chip], [kv_chip]
    for _ in range(chips - 1):
        small_steps.append(next_chip(small_steps[-1]))
        kv_steps.append(next_chip(kv_steps[-1]))
    kv_far = [other_block(kv, m) for kv in kv_steps for m in range(1, n_blk)]
    q_keep, q_give = call(
        turn_kernel, "turn", [shape(HEAD_SIZE, columns)] * 2, [queries], scalars=[core_here]
    )
    q_near = other_core(q_give)

    smalls = jnp.stack(small_steps)
    segs_own = smalls[:, :, 3 * top_count, :].reshape(2 * chips, tok)
    segs_far = [other_block(segs_own, m) for m in range(1, n_blk)]

    order_of = jnp.array(order, jnp.int32)
    place_of = jnp.array([order.index(z) for z in range(chips)], jnp.int32)
    chip_at = order_of[(place_of[chip] - jnp.arange(chips, dtype=jnp.int32)) % chips]
    core_at = jnp.stack([core, 1 - core]).astype(jnp.int32)
    device_at = (2 * chip_at[:, None] + core_at[None, :]).reshape(2 * chips)

    seg_q = segs_own[:2].astype(jnp.int32)
    table = jnp.arange(prefix_ids.shape[0], dtype=jnp.int32)
    pre_q = jnp.sum(
        jnp.where(seg_q[:, :, None] == table[None, None, :], prefix_ids[None, None, :], 0), axis=2
    )
    chip_start = (blk * n_uly + device_at[:2]) * tok

    def tile_info(segs, devices):
        segs = segs.astype(jnp.int32)
        low, high = segs[:, 0], segs[:, -1]
        needed = []
        for g in range(2):
            own = (low <= seg_q[g, -1]) & (high >= seg_q[g, 0])
            shared = jnp.any(
                (pre_q[g][None, :] >= low[:, None]) & (pre_q[g][None, :] <= high[:, None]), axis=1
            )
            needed.append((devices * tok <= chip_start[g]) & (own | shared))
        return jnp.concatenate([n.astype(jnp.int32) for n in needed] + [devices * tok, chip_start])

    seg_rows, pre_rows = seg_q.astype(F32)[:, None, :], pre_q.astype(F32)[:, None, :]
    state = attend(
        kv_steps,
        tile_info(segs_own, blk * n_uly + device_at),
        q_keep,
        q_near,
        seg_rows,
        pre_rows,
        segs_own.astype(F32)[:, None, :],
        None,
        False,
    )
    far_pieces = [(k, m) for k in range(chips) for m in range(1, n_blk)]
    far_segs = jnp.stack([s.reshape(chips, 2, tok) for s in segs_far], axis=1).reshape(-1, tok)
    far_blocks = jnp.stack([blk ^ m for m in range(1, n_blk)])
    far_devices = (
        far_blocks[None, :, None] * n_uly + device_at.reshape(chips, 1, 2)
    ).reshape(-1)
    attended, for_near = attend(
        kv_far,
        tile_info(far_segs, far_devices),
        q_keep,
        q_near,
        seg_rows,
        pre_rows,
        far_segs.astype(F32)[:, None, :],
        state,
        True,
    )
    mixed, normed = call(
        project_kernel,
        "project",
        [shape(tok, model_width, dtype=F32), shape(tok, model_width)],
        [attended, other_core(for_near), o_weight, hidden_in, post_gain[None, :]],
        scalars=[core_here],
        cost=(1_000_000_000, 9_000_000, 0),
    )

    capacity = max(2, 9 * tok * top_count // (8 * experts_all))
    slots = -(-2 * capacity // 8) * 8
    expert_of = jnp.stack([(blk ^ m) * n_uly + uly for m in range(n_blk)]).astype(BF16)
    kinds = smalls.reshape(chips, 2, 4, top_count, tok)
    named = kinds[:, :, 0, None] == expert_of[None, None, :, None, None]
    hit = jnp.any(named, axis=3)
    share_hi = jnp.sum(jnp.where(named, kinds[:, :, 1, None].astype(F32), 0.0), axis=3)
    share_lo = jnp.sum(jnp.where(named, kinds[:, :, 2, None].astype(F32), 0.0), axis=3)
    rank = jnp.dot(
        hit.astype(BF16).reshape(chips * 2 * n_blk, tok),
        jnp.triu(jnp.ones((tok, tok), BF16), 1),
        preferred_element_type=F32,
    ).reshape(chips, 2, n_blk, tok)
    rank = jnp.where(hit, rank + jnp.array([0.0, capacity], F32)[None, :, None, None], -1e6)

    def by_token(x):
        return x.transpose(0, 2, 1, 3).reshape(chips, n_blk, 2 * tok)

    rank, share_hi, share_lo = by_token(rank), by_token(share_hi), by_token(share_lo)
    rank_rows = rank.astype(jnp.int32)[:, :, None, :]
    first_slot = (jnp.arange(n_blk, dtype=jnp.int32) * slots).astype(F32)[None, :, None]
    place = jnp.concatenate(
        [jnp.where(rank >= 0.0, rank + first_slot, -1.0), share_hi, share_lo], axis=1
    ).transpose(0, 2, 1)

    picked = []
    rows_now = normed
    for k in range(chips):
        picked.append(
            call(
                functools.partial(pick_kernel, n_blk),
                "pick",
                [shape(slots, model_width)] * n_blk,
                [rows_now, other_core(rows_now), rank_rows[k]],
                cost=(300_000_000, 0, 0),
            )
        )
        if k < chips - 1:
            rows_now = next_chip(rows_now)
    answers = []
    for k in range(chips):
        inbox = [other_block(x, m) if m else x for m, x in enumerate(picked[k])]
        answers.append(
            call(
                functools.partial(expert_kernel, n_blk),
                "expert",
                [shape(slots, model_width)] * n_blk,
                [*inbox, w_gate[0], w_up[0], w_down[0]],
                scratch=[
                    pltpu.VMEM((n_blk * slots, model_width), BF16),
                    pltpu.VMEM((n_blk * slots, w_gate.shape[2]), BF16),
                ],
                unused=[picked[k + 1][0]] if k < chips - 1 else [],
                cost=(3_000_000_000, 0, 0),
            )
        )
    total = None
    for k in [*range(1, chips), 0]:
        back = [other_block(x, m) if m else x for m, x in enumerate(answers[k])]
        own, near = call(
            functools.partial(spread_kernel, n_blk),
            "spread",
            [shape(tok, model_width, dtype=F32), shape(tok, model_width)],
            [*back, place[k]],
            cost=(600_000_000, 0, 0),
        )
        partial = own + other_core(near).astype(F32)
        if total is not None:
            partial = partial + total.astype(F32)
        if k > 0:
            total = next_chip(partial.astype(BF16))
    return (mixed + partial).astype(BF16)


def solution(mesh):
    rows = P(("blk", "uly"), None)
    in_specs = (
        rows,
        rows,
        rows,
        rows,
        P(("blk", "uly")),
        P(),
        P(),
        P(),
        rows,
        rows,
        P(("blk", "uly"), None, None),
        P(("blk", "uly"), None, None),
        P(("blk", "uly"), None, None),
    )
    return jax.shard_map(shards, mesh=mesh, in_specs=in_specs, out_specs=rows, check_vma=False)
```

```python
import functools
import math

import jax
import jax.numpy as jnp
from jax import lax
from jax.experimental import pallas as pl
from jax.experimental.pallas import tpu as pltpu
from jax.sharding import PartitionSpec as P

HEAD_SIZE = 128
FLOOR = -1e20
HIDDEN = -1e30
BF16, F32 = jnp.bfloat16, jnp.float32


def chip_ring(count):
    return list(range(0, 1)) + list(range(1, count, 2)) + list(range(2, count, 2))[::-1]


def call(kernel, name, out_shape, operands, scalars=(), scratch=(), unused=(), vmem_mib=8):
    vmem = pl.BlockSpec(memory_space=pltpu.VMEM)
    several = isinstance(out_shape, (list, tuple))
    return pl.pallas_call(
        kernel,
        out_shape=out_shape,
        in_specs=[pl.BlockSpec(memory_space=pltpu.SMEM)] * len(scalars)
        + [vmem] * len(operands)
        + [pl.BlockSpec(memory_space=pl.ANY)] * len(unused),
        out_specs=[vmem] * len(out_shape) if several else vmem,
        scratch_shapes=list(scratch),
        compiler_params=pltpu.CompilerParams(vmem_limit_bytes=vmem_mib * 1024 * 1024),
        cost_estimate=pl.CostEstimate(flops=1000, bytes_accessed=1000, transcendentals=0),
        name=name,
    )(*scalars, *operands, *unused)


def message_kernel(core_ref, key_ref, value_ref, ids_ref, gates_ref, seg_ref, keep, give, small):
    first = core_ref[0] == 0
    k0, k1 = (key_ref[:, i * HEAD_SIZE : (i + 1) * HEAD_SIZE] for i in range(2))
    v0, v1 = (
        value_ref[:, i * HEAD_SIZE : (i + 1) * HEAD_SIZE].astype(F32).T.astype(BF16)
        for i in range(2)
    )
    keep[:, :HEAD_SIZE] = jnp.where(first, k0, k1)
    keep[:, HEAD_SIZE:] = jnp.where(first, v0, v1)
    give[:, :HEAD_SIZE] = jnp.where(first, k1, k0)
    give[:, HEAD_SIZE:] = jnp.where(first, v1, v0)
    share = gates_ref[...] / jnp.sum(gates_ref[...], axis=0, keepdims=True)
    share_hi = share.astype(BF16).astype(F32)
    segs = jnp.broadcast_to(seg_ref[...].astype(F32), share.shape)
    small[...] = jnp.concatenate(
        [ids_ref[...].astype(F32), share_hi, share - share_hi, segs], axis=0
    ).astype(BF16)


def turn_kernel(core_ref, query_ref, keep, give):
    first = core_ref[0] == 0
    half = keep.shape[1]
    tok = query_ref.shape[0]
    for h in range(half // tok):
        a, b = (
            query_ref[:, g * (half // tok) * HEAD_SIZE + h * HEAD_SIZE :][:, :HEAD_SIZE]
            .astype(F32)
            .T.astype(BF16)
            for g in range(2)
        )
        keep[:, h * tok : (h + 1) * tok] = jnp.where(first, a, b)
        give[:, h * tok : (h + 1) * tok] = jnp.where(first, b, a)


def attend_kernel(
    pieces, order, n_blk, first, last, where_ref, prefix_ref, segs_ref, q_own, q_near, pre_ref, *refs
):
    seg_ref, refs = refs[0], refs[1:]
    kv_refs, refs = refs[: len(pieces)], refs[len(pieces) :]
    if not first:
        top_in, sum_in, acc_in, *refs = refs
    if last:
        own_ref, near_ref, top_ref, sum_ref, acc_ref, q_ref = refs
    else:
        top_ref, sum_ref, acc_ref, q_ref = refs
    columns, rows = q_own.shape[1], pre_ref.shape[2]
    chips = len(order)
    scale = math.log2(math.e) / math.sqrt(HEAD_SIZE)
    width = 2 * rows
    q_ref[0] = q_own[...]
    q_ref[1] = q_near[...]
    if first:
        top_ref[...] = jnp.full_like(top_ref, FLOOR)
        sum_ref[...] = jnp.zeros_like(sum_ref)
        acc_ref[...] = jnp.zeros_like(acc_ref)
    else:
        top_ref[...] = top_in[...]
        sum_ref[...] = sum_in[...]
        acc_ref[...] = acc_in[...]
    blk, core, chip = where_ref[0], where_ref[1] % 2, where_ref[1] // 2
    place = sum(jnp.where(chip == z, i, 0) for i, z in enumerate(order))

    def start_of(k, m, j):
        at = lax.rem(place - k + chips, chips)
        chip_there = sum(jnp.where(at == i, z, 0) for i, z in enumerate(order))
        core_there = core + j - 2 * core * j
        return ((blk ^ m) * (2 * chips) + 2 * chip_there + core_there) * rows

    for kv_ref, (k, m) in zip(kv_refs, pieces, strict=True):

        def step(i, _, kv_ref=kv_ref, k=k, m=m):
            j, g = i // 2, i % 2
            tile = (k * n_blk + m) * 2 + j
            key_start, query_start = start_of(k, m, j), start_of(0, 0, g)
            low, high = segs_ref[tile, 0], segs_ref[tile, rows - 1]
            query_low, query_high = segs_ref[g, 0], segs_ref[g, rows - 1]

            def shared(s, found):
                prefix = prefix_ref[s]
                return found | ((prefix >= low) & (prefix <= high)).astype(jnp.int32)

            own = ((low <= query_high) & (high >= query_low)).astype(jnp.int32)
            seen = lax.fori_loop(query_low, query_high + 1, shared, own)

            @pl.when((seen > 0) & (key_start <= query_start))
            def _():
                square = (rows, rows)
                key_pos = key_start + lax.broadcasted_iota(jnp.int32, square, 0)
                query_pos = query_start + lax.broadcasted_iota(jnp.int32, square, 1)
                key_seg = jnp.broadcast_to(seg_ref[tile], square).T
                visible = (key_pos <= query_pos) & (
                    (key_seg == seg_ref[g]) | (key_seg == pre_ref[g])
                )
                bias = jnp.where(visible, 0.0, HIDDEN)
                bias = jnp.concatenate([bias] * (width // rows), axis=1)
                key_tile = kv_ref[j, :, :HEAD_SIZE]
                value_tile = kv_ref[j, :, HEAD_SIZE:]
                for at in range(0, columns, width):
                    part = pl.ds(at, width)
                    scores = (
                        jnp.dot(key_tile, q_ref[g, :, part], preferred_element_type=F32) * scale
                        + bias
                    )
                    old_top = top_ref[g, :, part]
                    new_top = jnp.maximum(old_top, jnp.max(scores, axis=0, keepdims=True))
                    weights = jnp.exp2(scores - new_top)
                    rescale = jnp.exp2(old_top - new_top)
                    top_ref[g, :, part] = new_top
                    sum_ref[g, :, part] = sum_ref[g, :, part] * rescale + jnp.sum(
                        weights, axis=0, keepdims=True
                    )
                    acc_ref[g, :, part] = acc_ref[g, :, part] * rescale + jnp.dot(
                        value_tile, weights.astype(BF16), preferred_element_type=F32
                    )

            return 0

        lax.fori_loop(0, 4, step, 0)
    if last:
        for g, out_ref in enumerate((own_ref, near_ref)):
            for h in range(columns // rows):
                part = pl.ds(h * rows, rows)
                result = acc_ref[g, :, part] / sum_ref[g, :, part]
                out_ref[:, h * HEAD_SIZE : (h + 1) * HEAD_SIZE] = result.T.astype(BF16)


def attend(kv_list, pieces, order, n_blk, scalars, q_own, q_near, pre_rows, seg_rows, state, last):
    head, columns = q_own.shape
    rows = pre_rows.shape[2]
    first = state is None
    state_shapes = [
        jax.ShapeDtypeStruct((2, 1, columns), F32),
        jax.ShapeDtypeStruct((2, 1, columns), F32),
        jax.ShapeDtypeStruct((2, head, columns), F32),
    ]
    scratch = [pltpu.VMEM((2, head, columns), BF16)]
    if last:
        out_shape = [jax.ShapeDtypeStruct((rows, columns // rows * head), BF16)] * 2
        scratch = [pltpu.VMEM(s.shape, s.dtype) for s in state_shapes] + scratch
    else:
        out_shape = state_shapes
    return call(
        functools.partial(attend_kernel, pieces, order, n_blk, first, last),
        "attend_last" if last else "attend_own",
        out_shape,
        [q_own, q_near, pre_rows, seg_rows, *kv_list, *(() if first else state)],
        scalars=scalars,
        scratch=scratch,
        vmem_mib=9 + len(kv_list) // 4,
    )


def project_kernel(core_ref, own_ref, got_ref, weight_ref, hidden_ref, gain_ref, mixed_ref, out_ref):
    core = core_ref[0]
    half = own_ref.shape[1]
    width = hidden_ref.shape[1]
    block = math.gcd(width, 512)
    own_at = pl.multiple_of(core * half, half)
    got_at = pl.multiple_of((1 - core) * half, half)

    def step(i, total):
        part = pl.ds(pl.multiple_of(i * block, block), block)
        now = (
            hidden_ref[:, part].astype(F32)
            + jnp.dot(
                own_ref[...], weight_ref[pl.ds(own_at, half), part], preferred_element_type=F32
            )
            + jnp.dot(
                got_ref[...], weight_ref[pl.ds(got_at, half), part], preferred_element_type=F32
            )
        )
        mixed_ref[:, part] = now
        return total + jnp.sum(now * now, axis=1, keepdims=True)

    total = lax.fori_loop(0, width // block, step, jnp.zeros((own_ref.shape[0], 1), F32))
    factor = lax.rsqrt(total / width + 1e-06)
    out_ref[...] = (mixed_ref[...] * factor * gain_ref[...]).astype(BF16)


def fetch_kernel(count, *refs):
    sources, targets, sems = refs[:count], refs[-count - 1 : -1], refs[-1]
    copies = [
        pltpu.make_async_copy(source, target, sems.at[i])
        for i, (source, target) in enumerate(zip(sources, targets, strict=True))
    ]
    for copy in copies:
        copy.start()
    for copy in copies:
        copy.wait()


def fetch(arrays, after):
    count = len(arrays)
    hbm = pl.BlockSpec(memory_space=pltpu.HBM)
    return pl.pallas_call(
        functools.partial(fetch_kernel, count),
        out_shape=[jax.ShapeDtypeStruct(x.shape, x.dtype) for x in arrays],
        in_specs=[hbm] * (count + len(after)),
        out_specs=[pl.BlockSpec(memory_space=pltpu.VMEM)] * count,
        scratch_shapes=[pltpu.SemaphoreType.DMA((count,))],
        compiler_params=pltpu.CompilerParams(vmem_limit_bytes=24 * 1024 * 1024),
        cost_estimate=pl.CostEstimate(flops=1000, bytes_accessed=1000, transcendentals=0),
        name="fetch",
    )(*arrays, *after)


def slots_kernel(top_count, capacity, pack, n_blk, n_uly, where_ref, *refs):
    chips = (len(refs) - 2) // 3
    smalls, ranks, places = refs[:chips], refs[chips : 2 * chips], refs[2 * chips : -2]
    unpack_ref, repack_ref = refs[-2:]
    tok = smalls[0].shape[2]
    targets = 2 * n_blk
    blk, uly = where_ref[0], where_ref[1]
    earlier = lax.broadcasted_iota(jnp.int32, (tok, tok), 0)
    before = jnp.where(earlier < lax.broadcasted_iota(jnp.int32, (tok, tok), 1), 1.0, 0.0)
    before = before.astype(BF16)
    for small_ref, rank_ref, place_ref in zip(smalls, ranks, places, strict=True):
        ids, hi, lo = (
            small_ref[0, i * top_count : (i + 1) * top_count, :].astype(F32) for i in range(3)
        )
        rows = [[], [], []]
        for target in range(targets):
            m, j = target // 2, target % 2
            named = ids == ((blk ^ m) * n_uly + (uly ^ j)).astype(F32)
            for at, x in enumerate((jnp.ones_like(ids), hi, lo)):
                rows[at].append(jnp.sum(jnp.where(named, x, 0.0), axis=0, keepdims=True))
        hit, hi, lo = (jnp.concatenate(r, axis=0) for r in rows)
        rank = jnp.dot(hit.astype(BF16), before, preferred_element_type=F32)
        rank = jnp.where(hit > 0.0, rank, -1e6)
        for target in range(targets):
            rank_ref[target] = rank[target : target + 1].astype(jnp.int32)
        first = lax.broadcasted_iota(jnp.int32, rank.shape, 0).astype(F32) * (capacity * pack)
        place = jnp.concatenate([rank + first, hi, lo], axis=0)
        spare = jnp.zeros((place_ref.shape[1] - place.shape[0], tok), F32)
        place_ref[...] = jnp.concatenate([place, spare], axis=0).T
    rows_all = targets * capacity
    for part in range(pack):
        for ref, row_axis in ((unpack_ref, 0), (repack_ref, 1)):
            dims = ref.shape[1:] if row_axis == 0 else (ref.shape[0], rows_all)
            row = lax.broadcasted_iota(jnp.int32, dims, row_axis)
            spot = lax.broadcasted_iota(jnp.int32, dims, 1 - row_axis)
            target = sum(jnp.where(row >= t * capacity, 1, 0) for t in range(1, targets))
            same = spot == row + target * (capacity * (pack - 1)) + part * capacity
            same = jnp.where(same, 1.0, 0.0).astype(BF16)
            if row_axis == 0:
                ref[part] = same
            else:
                ref[:, part * rows_all : (part + 1) * rows_all] = same


def pick_kernel(capacity, pack, x_ref, rank_ref, *refs):
    targets, tok = rank_ref.shape[0], x_ref.shape[0]
    outs = refs[-(targets // 2) :]
    _, slots, width = outs[0].shape
    slot = lax.broadcasted_iota(jnp.int32, (slots, tok), 0)
    chosen = jnp.concatenate(
        [
            jnp.concatenate(
                [jnp.where(rank_ref[t] + q * capacity == slot, 1.0, 0.0) for q in range(pack)], axis=1
            )
            for t in range(targets)
        ],
        axis=0,
    ).astype(BF16)
    block = math.gcd(width, 512)
    for at in range(0, width, block):
        parts = jnp.concatenate(
            [x_ref[:, q * width + at : q * width + at + block] for q in range(pack)], axis=0
        )
        rows = jnp.dot(chosen, parts, preferred_element_type=F32)
        for t in range(targets):
            outs[t // 2][t % 2, :, at : at + block] = rows[t * slots : (t + 1) * slots].astype(BF16)


def second_kernel(*refs):
    for i, ref in enumerate(refs[:-1]):
        refs[-1][i] = ref[1]


def join_kernel(n_blk, *refs):
    for m, out_ref in enumerate(refs[-n_blk:]):
        out_ref[0] = refs[m][...]
        out_ref[1] = refs[n_blk][m]


def expert_kernel(n_blk, pack, *refs):
    ins, other_ref, refs = refs[:n_blk], refs[n_blk], refs[n_blk + 1 :]
    gate_ref, up_ref, down_ref, unpack_ref, repack_ref = refs[:5]
    outs, other_out = refs[-n_blk - 5 : -5], refs[-5]
    mail_ref, rows_ref, act_ref, answer_ref = refs[-4:]
    mails = [r[0].astype(F32) for r in ins] + [other_ref[m].astype(F32) for m in range(n_blk)]
    _, slots, part_width = other_ref.shape
    rows_all = rows_ref.shape[0]
    mail_ref[...] = jnp.concatenate(mails, axis=0).astype(BF16)
    block = math.gcd(part_width, 512)
    for q in range(pack):
        for at in range(0, part_width, block):
            rows_ref[:, q * part_width + at : q * part_width + at + block] = jnp.dot(
                unpack_ref[q], mail_ref[:, at : at + block], preferred_element_type=F32
            ).astype(BF16)
    inner, width = down_ref.shape
    block = math.gcd(inner, 256)

    def hidden(i, _):
        part = pl.ds(pl.multiple_of(i * block, block), block)
        gate = jnp.dot(rows_ref[...], gate_ref[:, part], preferred_element_type=F32)
        up = jnp.dot(rows_ref[...], up_ref[:, part], preferred_element_type=F32)
        act_ref[:, part] = (gate / (1.0 + jnp.exp(-gate)) * up).astype(BF16)
        return 0

    lax.fori_loop(0, inner // block, hidden, 0)
    wide = math.gcd(part_width, 512)
    for q in range(pack):

        def answer(i, _, q=q):
            at = i * wide
            to = pl.ds(pl.multiple_of(at, wide), wide)
            part = pl.ds(pl.multiple_of(q * part_width + at, wide), wide)
            answer_ref[q * rows_all : (q + 1) * rows_all, to] = jnp.dot(
                act_ref[...], down_ref[:, part], preferred_element_type=F32
            ).astype(BF16)
            return 0

        lax.fori_loop(0, part_width // wide, answer, 0)
    for at in range(0, part_width, wide):
        mail = jnp.dot(
            repack_ref[...], answer_ref[:, at : at + wide], preferred_element_type=F32
        )
        for t in range(2 * n_blk):
            rows = mail[t * slots : (t + 1) * slots].astype(BF16)
            if t < n_blk:
                outs[t][:, at : at + wide] = rows
            else:
                other_out[t - n_blk, :, at : at + wide] = rows


def spread_kernel(targets, capacity, pack, added, *refs):
    n_blk = targets // 2
    backs, place_ref, adds = refs[:n_blk], refs[n_blk], refs[n_blk + 1 : n_blk + 1 + added]
    out_ref, mail_ref = refs[-2:]
    _, slots, part_width = backs[0].shape
    tok = out_ref.shape[0]
    mails = [r[j].astype(F32) for r in backs for j in range(2)]
    mail_ref[...] = jnp.concatenate(mails, axis=0).astype(BF16)
    place = place_ref[...]
    lane = lax.broadcasted_iota(jnp.int32, (tok, targets * slots), 1).astype(F32)
    for q in range(pack):
        weight_hi = jnp.zeros(lane.shape, F32)
        weight_lo = jnp.zeros(lane.shape, F32)
        for t in range(targets):
            hit = lane == place[:, t : t + 1] + q * capacity
            weight_hi = jnp.where(hit, place[:, targets + t : targets + t + 1], weight_hi)
            weight_lo = jnp.where(hit, place[:, 2 * targets + t : 2 * targets + t + 1], weight_lo)
        weight = jnp.concatenate([weight_hi, weight_lo], axis=0).astype(BF16)
        block = math.gcd(part_width, 512)
        for at in range(0, part_width, block):
            both = jnp.dot(weight, mail_ref[:, at : at + block], preferred_element_type=F32)
            to = slice(q * part_width + at, q * part_width + at + block)
            total = both[:tok] + both[tok:]
            for ref in adds:
                total = total + ref[:, to].astype(F32)
            out_ref[:, to] = total.astype(BF16)


def shards(
    hidden_in,
    queries,
    keys,
    values,
    segment_ids,
    prefix_ids,
    o_weight,
    post_gain,
    expert_ids,
    gates,
    w_gate,
    w_up,
    w_down,
):
    tok, model_width = hidden_in.shape
    n_blk, n_uly = lax.axis_size("blk"), lax.axis_size("uly")
    chips = n_uly // 2
    experts_all = n_blk * n_uly
    top_count = expert_ids.shape[1]
    columns = queries.shape[1] // HEAD_SIZE // 2 * tok
    blk, uly = lax.axis_index("blk"), lax.axis_index("uly")
    core, chip = uly % 2, uly // 2
    me = blk * n_uly + uly
    core_here = core.astype(jnp.int32)[None]

    order = chip_ring(chips)
    ring_pairs = [
        (2 * order[i] + c, 2 * order[(i + 1) % chips] + c) for i in range(chips) for c in range(2)
    ]
    swap_pairs = [(u, u ^ 1) for u in range(n_uly)]
    next_chip = functools.partial(lax.ppermute, axis_name="uly", perm=ring_pairs)
    other_core = functools.partial(lax.ppermute, axis_name="uly", perm=swap_pairs)

    def other_block(x, m):
        return lax.ppermute(x, "blk", [(b, b ^ m) for b in range(n_blk)])

    def shape(*dims, dtype=BF16):
        return jax.ShapeDtypeStruct(dims, dtype)

    keep, give, small = call(
        message_kernel,
        "message",
        [shape(tok, 2 * HEAD_SIZE), shape(tok, 2 * HEAD_SIZE), shape(4 * top_count, tok)],
        [keys, values, expert_ids.T, gates.T, segment_ids[None, :]],
        scalars=[core_here],
    )
    kv_chip = jnp.stack([keep, other_core(give)])
    kv_chip, small = lax.optimization_barrier((kv_chip, small))
    small_chip = jnp.stack([small, other_core(small)])
    seg_at = 3 * top_count
    segs_chip = small_chip[:, seg_at : seg_at + 1]
    small_steps, kv_steps, kv_far = [], [kv_chip], []
    for k in range(chips):
        kv_far += [other_block(kv_steps[k], m) for m in range(1, n_blk)]
        if k < chips - 1:
            kv_next = next_chip(kv_steps[k])
            if k > 0:
                small_steps.append(next_chip(small_steps[-1]))
                sent = n_blk - 1
                kv_next, small_steps[-1], *kv_far[-2 * sent : -sent] = lax.optimization_barrier(
                    (kv_next, small_steps[-1], *kv_far[-2 * sent : -sent])
                )
            else:
                segs_plane = [other_block(small_chip[:, seg_at:], m)[:, :1] for m in range(1, n_blk)]
                kv_next, *segs_plane = lax.optimization_barrier((kv_next, *segs_plane))
                small_chip = jnp.concatenate([small_chip[:, :seg_at], segs_chip, *segs_plane], axis=1)
                small_chip = jnp.pad(small_chip, ((0, 0), (0, -small_chip.shape[1] % 16), (0, 0)))
                small_steps.append(small_chip)
            kv_steps.append(kv_next)
        else:
            small_steps.append(next_chip(small_steps[-1]))
    q_keep, q_give = call(
        turn_kernel, "turn", [shape(HEAD_SIZE, columns)] * 2, [queries], scalars=[core_here]
    )
    q_near = other_core(q_give)

    capacity = max(2, 9 * tok * top_count // (8 * experts_all))
    pack = 8 // math.gcd(capacity, 8)
    slots, part_width = capacity * pack, model_width // pack
    targets = 2 * n_blk
    rows_all = targets * capacity
    where = jnp.stack([blk, uly]).astype(jnp.int32)
    slot_tables = call(
        functools.partial(slots_kernel, top_count, capacity, pack, n_blk, n_uly),
        "slots",
        [shape(targets, 1, tok, dtype=jnp.int32)] * chips
        + [shape(tok, 128, dtype=F32)] * chips
        + [shape(pack, rows_all, targets * slots), shape(targets * slots, pack * rows_all)],
        small_steps,
        scalars=[where],
    )
    ranks, place, unpack, repack = (
        slot_tables[:chips],
        slot_tables[chips : 2 * chips],
        slot_tables[-2],
        slot_tables[-1],
    )
    o_here, gate_here, up_here, down_here = fetch(
        [o_weight, w_gate[0], w_up[0], w_down[0]], [kv_steps[-2]]
    )

    smalls = jnp.stack(small_steps)
    segs = smalls[:, :, seg_at : seg_at + n_blk].transpose(0, 2, 1, 3).reshape(-1, tok)
    seg_rows = segs.astype(F32)[:, None, :]
    segs = segs.astype(jnp.int32)
    table = jnp.arange(prefix_ids.shape[0], dtype=jnp.int32)
    pre_q = jnp.sum(
        jnp.where(segs[:2, :, None] == table[None, None, :], prefix_ids[None, None, :], 0), axis=2
    )
    pre_rows = pre_q.astype(F32)[:, None, :]
    scalars = [where, prefix_ids, segs]
    early = [seg_rows, o_here, gate_here, up_here, down_here, unpack, repack, *ranks, *place]
    seg_rows, o_here, gate_here, up_here, down_here, unpack, repack, *early = (
        lax.optimization_barrier(early)
    )
    ranks, place = early[:chips], early[chips:]
    state = attend(
        kv_steps,
        [(k, 0) for k in range(chips)],
        order,
        n_blk,
        scalars,
        q_keep,
        q_near,
        pre_rows,
        seg_rows,
        None,
        False,
    )
    attended, for_near = attend(
        kv_far,
        [(k, m) for k in range(chips) for m in range(1, n_blk)],
        order,
        n_blk,
        scalars,
        q_keep,
        q_near,
        pre_rows,
        seg_rows,
        state,
        True,
    )
    mixed, normed = call(
        project_kernel,
        "project",
        [shape(tok, model_width, dtype=F32), shape(tok, model_width)],
        [attended, other_core(for_near), o_here, hidden_in, post_gain[None, :]],
        scalars=[core_here],
        vmem_mib=10,
    )

    part = shape(slots, part_width)
    halves, stacked = shape(2, slots, part_width), shape(n_blk, slots, part_width)

    def pick(k, rows):
        kernel = functools.partial(pick_kernel, capacity, pack)
        return call(kernel, "pick", [halves] * n_blk, [rows, ranks[k]])

    def expert(inbox, swapped):
        *own, other = call(
            functools.partial(expert_kernel, n_blk, pack),
            "expert",
            [part] * n_blk + [stacked],
            [*inbox, swapped, gate_here, up_here, down_here, unpack, repack],
            scratch=[
                pltpu.VMEM((targets * slots, part_width), BF16),
                pltpu.VMEM((rows_all, model_width), BF16),
                pltpu.VMEM((rows_all, w_gate.shape[2]), BF16),
                pltpu.VMEM((pack * rows_all, part_width), BF16),
            ],
            vmem_mib=12,
        )
        return own, other

    def spread(k, back, adds):
        return call(
            functools.partial(spread_kernel, targets, capacity, pack, len(adds)),
            "spread",
            shape(tok, model_width),
            [*back, place[k], *adds],
            scratch=[pltpu.VMEM((targets * slots, part_width), BF16)],
            vmem_mib=4 * pack,
        )

    def exchange(parts):
        return [other_block(x, m) if m else x for m, x in enumerate(parts)]

    way_back = [*range(1, chips), 0]
    rows, outbox = {0: normed}, {0: pick(0, normed)}
    arrived, own, other, got, back, total = {}, {}, {}, {}, {}, {}
    for now in range(2 * chips):
        new = {}
        if now + 1 < chips:
            new["rows", now + 1] = [next_chip(rows[now])]
        if now < chips:
            new["arrived", now] = exchange(outbox[now])
        if now >= chips:
            k = way_back[now - chips]
            joined = call(
                functools.partial(join_kernel, n_blk), "join", [halves] * n_blk, [*own[k], got[k]]
            )
            new["back", k] = exchange(joined)
        if now > chips:
            k = way_back[now - chips - 1]
            before = [total[way_back[now - chips - 2]]] if now > chips + 1 else []
            new["total", k] = [next_chip(spread(k, back[k], before))]
        if chips - 1 <= now < 2 * chips - 1:
            k = way_back[now - chips + 1]
            new["got", k] = [other_core(other[k])]
        if 1 <= now <= chips:
            k = now - 1
            seconds = call(second_kernel, "second", stacked, arrived[k])
            own_k, other_k = expert(arrived[k], other_core(seconds))
            new["own", k], new["other", k] = own_k, [other_k]
        if now + 1 < chips:
            new["outbox", now + 1] = pick(now + 1, new["rows", now + 1][0])
        flat = lax.optimization_barrier([x for group in new.values() for x in group])
        for (kind, k), group in new.items():
            group = [flat.pop(0) for _ in group]
            for name, table in (("arrived", arrived), ("own", own), ("back", back), ("outbox", outbox)):
                if kind == name:
                    table[k] = group
            for name, table in (("rows", rows), ("other", other), ("got", got), ("total", total)):
                if kind == name:
                    table[k] = group[0]
    before = [total[way_back[-2]]] if chips > 1 else []
    return spread(0, back[0], [*before, mixed])


def solution(mesh):
    rows = P(("blk", "uly"), None)
    in_specs = (
        rows,
        rows,
        rows,
        rows,
        P(("blk", "uly")),
        P(),
        P(),
        P(),
        rows,
        rows,
        P(("blk", "uly"), None, None),
        P(("blk", "uly"), None, None),
        P(("blk", "uly"), None, None),
    )
    return jax.shard_map(shards, mesh=mesh, in_specs=in_specs, out_specs=rows, check_vma=False)
```

```python
import functools
import math

import jax
import jax.numpy as jnp
from jax import lax
from jax.experimental import pallas as pl
from jax.experimental.pallas import tpu as pltpu
from jax.sharding import PartitionSpec as P

HEAD_SIZE = 128
FLOOR = -1e20
HIDDEN = -1e30
BF16, F32 = jnp.bfloat16, jnp.float32


def chip_ring(count):
    return list(range(0, 1)) + list(range(1, count, 2)) + list(range(2, count, 2))[::-1]


def call(
    kernel, name, out_shape, operands, scalars=(), scratch=(), unused=(), vmem_mib=4, flops=1000
):
    vmem = pl.BlockSpec(memory_space=pltpu.VMEM)
    several = isinstance(out_shape, (list, tuple))
    return pl.pallas_call(
        kernel,
        out_shape=out_shape,
        in_specs=[pl.BlockSpec(memory_space=pltpu.SMEM)] * len(scalars)
        + [vmem] * len(operands)
        + [pl.BlockSpec(memory_space=pl.ANY)] * len(unused),
        out_specs=[vmem] * len(out_shape) if several else vmem,
        scratch_shapes=list(scratch),
        compiler_params=pltpu.CompilerParams(vmem_limit_bytes=vmem_mib * 1024 * 1024),
        cost_estimate=pl.CostEstimate(flops=flops, bytes_accessed=1000, transcendentals=0),
        name=name,
    )(*scalars, *operands, *unused)


def message_kernel(core_ref, key_ref, value_ref, ids_ref, gates_ref, seg_ref, keep, give):
    tok = key_ref.shape[0]
    first = core_ref[0] == 0
    k0, k1 = (key_ref[:, i * HEAD_SIZE : (i + 1) * HEAD_SIZE] for i in range(2))
    v0, v1 = (
        value_ref[:, i * HEAD_SIZE : (i + 1) * HEAD_SIZE].astype(F32).T.astype(BF16)
        for i in range(2)
    )
    share = gates_ref[...] / jnp.sum(gates_ref[...], axis=0, keepdims=True)
    share_hi = share.astype(BF16).astype(F32)
    segs = jnp.broadcast_to(seg_ref[...].astype(F32), share.shape)
    left = jnp.concatenate([ids_ref[...].astype(F32), share_hi], axis=0)
    right = jnp.concatenate([share - share_hi, segs], axis=0)
    small = jnp.concatenate([left, right], axis=1).astype(BF16)
    keep[:tok, :HEAD_SIZE] = jnp.where(first, k0, k1)
    keep[:tok, HEAD_SIZE:] = jnp.where(first, v0, v1)
    keep[tok:, :] = small
    give[:tok, :HEAD_SIZE] = jnp.where(first, k1, k0)
    give[:tok, HEAD_SIZE:] = jnp.where(first, v1, v0)
    give[tok:, :] = small


def small_part(ref, j, tok):
    rows = ref[j, tok:, :].astype(F32)
    half = rows.shape[0] // 2
    return rows[:half, :tok], rows[half:, :tok], rows[:half, tok:], rows[half : half + 1, tok:]


def pair_kernel(a_ref, b_ref, out_ref):
    if len(a_ref.shape) < len(out_ref.shape):
        out_ref[0] = a_ref[...]
        out_ref[1] = b_ref[...]
    else:
        out_ref[: a_ref.shape[0]] = a_ref[...]
        out_ref[a_ref.shape[0] :] = b_ref[...]


def turn_kernel(core_ref, query_ref, keep, give):
    first = core_ref[0] == 0
    half = keep.shape[1]
    tok = query_ref.shape[0]
    for h in range(half // tok):
        a, b = (
            query_ref[:, g * (half // tok) * HEAD_SIZE + h * HEAD_SIZE :][:, :HEAD_SIZE]
            .astype(F32)
            .T.astype(BF16)
            for g in range(2)
        )
        keep[:, h * tok : (h + 1) * tok] = jnp.where(first, a, b)
        give[:, h * tok : (h + 1) * tok] = jnp.where(first, b, a)


def attend_kernel(
    pieces, order, n_blk, first, last, where_ref, prefix_ref, q_own, q_near, home_ref, *refs
):
    kv_refs, refs = refs[: len(pieces)], refs[len(pieces) :]
    if not first:
        top_in, sum_in, acc_in, *refs = refs
    if last:
        own_ref, near_ref, top_ref, sum_ref, acc_ref, *refs = refs
    else:
        top_ref, sum_ref, acc_ref, *refs = refs
    seg_ref, pre_ref, table, segs_ref, sem, q_ref = refs
    columns, rows = q_own.shape[1], home_ref.shape[1] - 16
    each = kv_refs[0].shape[0]
    for tile in range(2 + each * len(pieces)):
        ref, at = (home_ref, tile) if tile < 2 else (kv_refs[(tile - 2) // each], (tile - 2) % each)
        seg_ref[tile] = small_part(ref, at, rows)[3]
        table[tile : tile + 1, :] = seg_ref[tile].astype(jnp.int32)
    copy = pltpu.make_async_copy(table, segs_ref, sem)
    copy.start()
    copy.wait()
    for g in range(2):

        def prefixes(s, row, g=g):
            return jnp.where(seg_ref[g] == s.astype(F32), prefix_ref[s].astype(F32), row)

        pre_ref[g] = lax.fori_loop(
            segs_ref[g, 0], segs_ref[g, rows - 1] + 1, prefixes, jnp.zeros((1, rows), F32)
        )
    chips = len(order)
    scale = math.log2(math.e) / math.sqrt(HEAD_SIZE)
    width = 2 * rows
    q_ref[0] = q_own[...]
    q_ref[1] = q_near[...]
    if first:
        top_ref[...] = jnp.full_like(top_ref, FLOOR)
        sum_ref[...] = jnp.zeros_like(sum_ref)
        acc_ref[...] = jnp.zeros_like(acc_ref)
    else:
        top_ref[...] = top_in[...]
        sum_ref[...] = sum_in[...]
        acc_ref[...] = acc_in[...]
    blk, core, chip = where_ref[0], where_ref[1] % 2, where_ref[1] // 2
    place = sum(jnp.where(chip == z, i, 0) for i, z in enumerate(order))

    def start_of(k, m, j):
        at = lax.rem(place - k + chips, chips)
        chip_there = sum(jnp.where(at == i, z, 0) for i, z in enumerate(order))
        core_there = core + j - 2 * core * j
        return ((blk ^ m) * (2 * chips) + 2 * chip_there + core_there) * rows

    for number, (kv_ref, (k, m)) in enumerate(zip(kv_refs, pieces, strict=True)):

        def step(i, _, number=number, kv_ref=kv_ref, k=k, m=m):
            at, g = i // 2, i % 2
            tile = 2 + each * number + at
            key_start, query_start = start_of(k + at // 2, m, at % 2), start_of(0, 0, g)
            low, high = segs_ref[tile, 0], segs_ref[tile, rows - 1]
            query_low, query_high = segs_ref[g, 0], segs_ref[g, rows - 1]

            def shared(s, found):
                prefix = prefix_ref[s]
                return found | ((prefix >= low) & (prefix <= high)).astype(jnp.int32)

            own = ((low <= query_high) & (high >= query_low)).astype(jnp.int32)
            seen = lax.fori_loop(query_low, query_high + 1, shared, own)

            @pl.when((seen > 0) & (key_start <= query_start))
            def _():
                square = (rows, rows)
                key_pos = key_start + lax.broadcasted_iota(jnp.int32, square, 0)
                query_pos = query_start + lax.broadcasted_iota(jnp.int32, square, 1)
                key_seg = jnp.broadcast_to(seg_ref[tile], square).T
                visible = (key_pos <= query_pos) & (
                    (key_seg == seg_ref[g]) | (key_seg == pre_ref[g])
                )
                bias = jnp.where(visible, 0.0, HIDDEN)
                bias = jnp.concatenate([bias] * (width // rows), axis=1)
                key_tile = kv_ref[at, :rows, :HEAD_SIZE]
                value_tile = kv_ref[at, :rows, HEAD_SIZE:]
                for column in range(0, columns, width):
                    part = pl.ds(column, width)
                    scores = (
                        jnp.dot(key_tile, q_ref[g, :, part], preferred_element_type=F32) * scale
                        + bias
                    )
                    old_top = top_ref[g, :, part]
                    new_top = jnp.maximum(old_top, jnp.max(scores, axis=0, keepdims=True))
                    weights = jnp.exp2(scores - new_top)
                    rescale = jnp.exp2(old_top - new_top)
                    top_ref[g, :, part] = new_top
                    sum_ref[g, :, part] = sum_ref[g, :, part] * rescale + jnp.sum(
                        weights, axis=0, keepdims=True
                    )
                    acc_ref[g, :, part] = acc_ref[g, :, part] * rescale + jnp.dot(
                        value_tile, weights.astype(BF16), preferred_element_type=F32
                    )

            return 0

        lax.fori_loop(0, 2 * each, step, 0)
    if last:
        for g, out_ref in enumerate((own_ref, near_ref)):
            for h in range(columns // rows):
                part = pl.ds(h * rows, rows)
                result = acc_ref[g, :, part] / sum_ref[g, :, part]
                out_ref[:, h * HEAD_SIZE : (h + 1) * HEAD_SIZE] = result.T.astype(BF16)


def attend(kv_list, pieces, order, n_blk, scalars, q_own, q_near, home, state, last):
    head, columns = q_own.shape
    rows = home.shape[1] - 16
    tiles = 2 + kv_list[0].shape[0] * len(kv_list)
    first = state is None
    state_shapes = [
        jax.ShapeDtypeStruct((2, 1, columns), F32),
        jax.ShapeDtypeStruct((2, 1, columns), F32),
        jax.ShapeDtypeStruct((2, head, columns), F32),
    ]
    scratch = [
        pltpu.VMEM((tiles, 1, rows), F32),
        pltpu.VMEM((2, 1, rows), F32),
        pltpu.VMEM((tiles, rows), jnp.int32),
        pltpu.SMEM((tiles, rows), jnp.int32),
        pltpu.SemaphoreType.DMA,
        pltpu.VMEM((2, head, columns), BF16),
    ]
    if last:
        out_shape = [jax.ShapeDtypeStruct((rows, columns // rows * head), BF16)] * 2
        scratch = [pltpu.VMEM(s.shape, s.dtype) for s in state_shapes] + scratch
    else:
        out_shape = state_shapes
    return call(
        functools.partial(attend_kernel, pieces, order, n_blk, first, last),
        "attend_last" if last else "attend_own",
        out_shape,
        [q_own, q_near, home, *kv_list, *(() if first else state)],
        scalars=scalars,
        scratch=scratch,
        vmem_mib=5 + len(kv_list) // 2,
        flops=8_000_000_000 if last else 1000,
    )


def project_kernel(
    core_ref, own_ref, got_ref, hidden_ref, gain_ref, weight_hbm, mixed_ref, out_ref, weight_ref, sems
):
    core = core_ref[0]
    half = own_ref.shape[1]
    width = hidden_ref.shape[1]
    blocks = sems.shape[0]
    block = width // blocks
    own_at = pl.multiple_of(core * half, half)
    got_at = pl.multiple_of((1 - core) * half, half)
    copies = [
        pltpu.make_async_copy(
            weight_hbm.at[:, pl.ds(i * block, block)], weight_ref.at[i], sems.at[i]
        )
        for i in range(blocks)
    ]
    for copy in copies:
        copy.start()
    total = jnp.zeros((own_ref.shape[0], 1), F32)
    for i, copy in enumerate(copies):
        part = pl.ds(i * block, block)
        copy.wait()
        now = (
            hidden_ref[:, part].astype(F32)
            + jnp.dot(
                own_ref[...], weight_ref[i, pl.ds(own_at, half), :], preferred_element_type=F32
            )
            + jnp.dot(
                got_ref[...], weight_ref[i, pl.ds(got_at, half), :], preferred_element_type=F32
            )
        )
        mixed_ref[:, part] = now
        total = total + jnp.sum(now * now, axis=1, keepdims=True)
    factor = lax.rsqrt(total / width + 1e-06)
    out_ref[...] = (mixed_ref[...] * factor * gain_ref[...]).astype(BF16)


def fetch_kernel(count, *refs):
    sources, targets, sems = refs[:count], refs[-count - 1 : -1], refs[-1]
    copies = [
        pltpu.make_async_copy(source, target, sems.at[i])
        for i, (source, target) in enumerate(zip(sources, targets, strict=True))
    ]
    for copy in copies:
        copy.start()
    for copy in copies:
        copy.wait()


def fetch(arrays, after):
    count = len(arrays)
    hbm = pl.BlockSpec(memory_space=pltpu.HBM)
    return pl.pallas_call(
        functools.partial(fetch_kernel, count),
        out_shape=[jax.ShapeDtypeStruct(x.shape, x.dtype) for x in arrays],
        in_specs=[hbm] * (count + len(after)),
        out_specs=[pl.BlockSpec(memory_space=pltpu.VMEM)] * count,
        scratch_shapes=[pltpu.SemaphoreType.DMA((count,))],
        compiler_params=pltpu.CompilerParams(vmem_limit_bytes=4 * 1024 * 1024),
        cost_estimate=pl.CostEstimate(flops=1000, bytes_accessed=1000, transcendentals=0),
        name="fetch",
    )(*arrays, *after)


def sort_rows(kv_ref, where_ref, top_count, n_blk, n_uly):
    tok = kv_ref.shape[1] - 16
    blk, uly = where_ref[0], where_ref[1]
    ids, hi, lo, _ = (x[:top_count] for x in small_part(kv_ref, 0, tok))
    rows = [[], [], []]
    for target in range(2 * n_blk):
        m, j = target // 2, target % 2
        named = ids == ((blk ^ m) * n_uly + (uly ^ j)).astype(F32)
        for at, x in enumerate((jnp.ones_like(ids), hi, lo)):
            rows[at].append(jnp.sum(jnp.where(named, x, 0.0), axis=0, keepdims=True))
    hit, hi, lo = (jnp.concatenate(r, axis=0) for r in rows)
    earlier = lax.broadcasted_iota(jnp.int32, (tok, tok), 0)
    before = jnp.where(earlier < lax.broadcasted_iota(jnp.int32, (tok, tok), 1), 1.0, 0.0)
    rank = jnp.dot(hit.astype(BF16), before.astype(BF16), preferred_element_type=F32)
    return jnp.where(hit > 0.0, rank, -1e6), hi, lo


def weights_kernel(top_count, capacity, pack, n_blk, n_uly, where_ref, *refs):
    chips = (len(refs) - 1) // 2
    targets, slots = 2 * n_blk, capacity * pack
    for kv_ref, weight_ref in zip(refs[:chips], refs[-chips:], strict=True):
        tok = kv_ref.shape[1] - 16
        rank, hi, lo = sort_rows(kv_ref, where_ref, top_count, n_blk, n_uly)
        first = lax.broadcasted_iota(jnp.int32, rank.shape, 0).astype(F32) * slots
        spare = jnp.zeros((tok - 3 * targets, tok), F32)
        place = jnp.concatenate([rank + first, hi, lo, spare], axis=0).T
        for q in range(pack):
            for at in range(0, targets * slots, 128):
                width = min(128, targets * slots - at)
                lane = at + lax.broadcasted_iota(jnp.int32, (tok, width), 1).astype(F32)
                weight_hi = jnp.zeros(lane.shape, F32)
                weight_lo = jnp.zeros(lane.shape, F32)
                for t in range(at // slots, min(targets, -(-(at + width) // slots))):
                    hit = lane == place[:, t : t + 1] + q * capacity
                    weight_hi = jnp.where(hit, place[:, targets + t : targets + t + 1], weight_hi)
                    weight_lo = jnp.where(
                        hit, place[:, 2 * targets + t : 2 * targets + t + 1], weight_lo
                    )
                weight_ref[q, :tok, at : at + width] = weight_hi.astype(BF16)
                weight_ref[q, tok:, at : at + width] = weight_lo.astype(BF16)


def slots_kernel(top_count, capacity, pack, n_blk, n_uly, where_ref, *refs):
    chips = (len(refs) - 2) // 2
    unpack_ref, repack_ref = refs[-2:]
    targets = 2 * n_blk
    for kv_ref, rank_ref in zip(refs[:chips], refs[chips:-2], strict=True):
        rank = sort_rows(kv_ref, where_ref, top_count, n_blk, n_uly)[0].astype(jnp.int32)
        for target in range(targets):
            rank_ref[target] = rank[target : target + 1]
    for part in range(pack):
        for ref, row_axis in ((unpack_ref, 0), (repack_ref, 1)):
            row = lax.broadcasted_iota(jnp.int32, ref.shape[1:], row_axis)
            spot = lax.broadcasted_iota(jnp.int32, ref.shape[1:], 1 - row_axis)
            target = sum(jnp.where(row >= t * capacity, 1, 0) for t in range(1, n_blk))
            same = spot == row + target * (capacity * (pack - 1)) + part * capacity
            ref[part] = jnp.where(same, 1.0, 0.0).astype(BF16)


def pick_kernel(capacity, pack, x_ref, rank_ref, *refs):
    targets, tok = rank_ref.shape[0], x_ref.shape[0]
    outs = refs[-(targets // 2) :]
    _, slots, width = outs[0].shape
    slot = lax.broadcasted_iota(jnp.int32, (slots, tok), 0)
    chosen = jnp.concatenate(
        [
            jnp.concatenate(
                [jnp.where(rank_ref[t] + q * capacity == slot, 1.0, 0.0) for q in range(pack)], axis=1
            )
            for t in range(targets)
        ],
        axis=0,
    ).astype(BF16)
    block = math.gcd(width, 512)
    for at in range(0, width, block):
        parts = jnp.concatenate(
            [x_ref[:, q * width + at : q * width + at + block] for q in range(pack)], axis=0
        )
        rows = jnp.dot(chosen, parts, preferred_element_type=F32)
        for t in range(targets):
            outs[t // 2][t % 2, :, at : at + block] = rows[t * slots : (t + 1) * slots].astype(BF16)


def expert_kernel(n_blk, pack, *refs):
    ins, experts, (unpack_ref, repack_ref), refs = (
        refs[:n_blk],
        (refs[n_blk : n_blk + 3], refs[n_blk + 3 : n_blk + 6]),
        refs[n_blk + 6 : n_blk + 8],
        refs[n_blk + 8 :],
    )
    outs, (mail_ref, rows_ref, act_ref, answer_ref) = refs[-n_blk - 4 : -4], refs[-4:]
    _, slots, part_width = ins[0].shape
    block = math.gcd(part_width, 512)
    for j, (gate_ref, up_ref, down_ref) in enumerate(experts):
        mail_ref[j] = jnp.concatenate([r[j].astype(F32) for r in ins], axis=0).astype(BF16)
        for q in range(pack):
            for at in range(0, part_width, block):
                rows_ref[j, :, q * part_width + at : q * part_width + at + block] = jnp.dot(
                    unpack_ref[q], mail_ref[j, :, at : at + block], preferred_element_type=F32
                ).astype(BF16)
        inner = down_ref.shape[1]
        inner_block = math.gcd(inner, 256)

        def hidden(i, _, j=j, gate_ref=gate_ref, up_ref=up_ref):
            part = pl.ds(pl.multiple_of(i * inner_block, inner_block), inner_block)
            gate = jnp.dot(rows_ref[j], gate_ref[0, :, part], preferred_element_type=F32)
            up = jnp.dot(rows_ref[j], up_ref[0, :, part], preferred_element_type=F32)
            act_ref[j, :, part] = (gate / (1.0 + jnp.exp(-gate)) * up).astype(BF16)
            return 0

        lax.fori_loop(0, inner // inner_block, hidden, 0)
        for q in range(pack):

            def answer(i, _, j=j, q=q, down_ref=down_ref):
                at = i * block
                to = pl.ds(pl.multiple_of(at, block), block)
                part = pl.ds(pl.multiple_of(q * part_width + at, block), block)
                answer_ref[j, q, :, to] = jnp.dot(
                    act_ref[j], down_ref[0, :, part], preferred_element_type=F32
                ).astype(BF16)
                return 0

            lax.fori_loop(0, part_width // block, answer, 0)
        for at in range(0, part_width, block):
            mail = sum(
                jnp.dot(
                    repack_ref[q],
                    answer_ref[j, q, :, at : at + block],
                    preferred_element_type=F32,
                )
                for q in range(pack)
            )
            for m in range(n_blk):
                outs[m][j, :, at : at + block] = mail[m * slots : (m + 1) * slots].astype(BF16)


def spread_kernel(n_blk, pack, added, *refs):
    backs, weight_ref, adds = refs[:n_blk], refs[n_blk], refs[n_blk + 1 : n_blk + 1 + added]
    out_ref, mail_ref = refs[-2:]
    _, slots, part_width = backs[0].shape
    tok = out_ref.shape[0]
    mails = [r[j].astype(F32) for r in backs for j in range(2)]
    mail_ref[...] = jnp.concatenate(mails, axis=0).astype(BF16)
    block = math.gcd(part_width, 512)
    for q in range(pack):
        for at in range(0, part_width, block):
            both = jnp.dot(weight_ref[q], mail_ref[:, at : at + block], preferred_element_type=F32)
            to = slice(q * part_width + at, q * part_width + at + block)
            total = both[:tok] + both[tok:]
            for ref in adds:
                total = total + ref[:, to].astype(F32)
            out_ref[:, to] = total.astype(BF16)


def shards(
    hidden_in,
    queries,
    keys,
    values,
    segment_ids,
    prefix_ids,
    o_weight,
    post_gain,
    expert_ids,
    gates,
    w_gate,
    w_up,
    w_down,
):
    tok, model_width = hidden_in.shape
    n_blk, n_uly = lax.axis_size("blk"), lax.axis_size("uly")
    chips = n_uly // 2
    experts_all = n_blk * n_uly
    top_count = expert_ids.shape[1]
    columns = queries.shape[1] // HEAD_SIZE // 2 * tok
    blk, uly = lax.axis_index("blk"), lax.axis_index("uly")
    core, chip = uly % 2, uly // 2
    me = blk * n_uly + uly
    core_here = core.astype(jnp.int32)[None]

    order = chip_ring(chips)
    ring_pairs = [
        (2 * order[i] + c, 2 * order[(i + 1) % chips] + c) for i in range(chips) for c in range(2)
    ]
    swap_pairs = [(u, u ^ 1) for u in range(n_uly)]
    next_chip = functools.partial(lax.ppermute, axis_name="uly", perm=ring_pairs)
    other_core = functools.partial(lax.ppermute, axis_name="uly", perm=swap_pairs)

    def other_block(x, m):
        return lax.ppermute(x, "blk", [(b, b ^ m) for b in range(n_blk)])

    def tied(*groups):
        flat = list(lax.optimization_barrier(tuple(x for group in groups for x in group)))
        return [[flat.pop(0) for _ in group] for group in groups]

    def shape(*dims, dtype=BF16):
        return jax.ShapeDtypeStruct(dims, dtype)

    keep, give = call(
        message_kernel,
        "message",
        [shape(tok + 16, 2 * HEAD_SIZE)] * 2,
        [keys, values, expert_ids.T, gates.T, segment_ids[None, :]],
        scalars=[core_here],
    )
    where = jnp.stack([blk, uly]).astype(jnp.int32)
    q_keep, q_give = call(
        turn_kernel, "turn", [shape(HEAD_SIZE, columns)] * 2, [queries], scalars=[core_here]
    )
    kv_steps = [
        call(pair_kernel, "pair", shape(2, tok + 16, 2 * HEAD_SIZE), [keep, other_core(give)])
    ]
    groups, kv_far = [], []
    for k in range(1, chips):
        kv_next = next_chip(kv_steps[-1])
        beside = [q_keep, other_core(q_give)] if k == 1 else []
        kv_next, *beside = lax.optimization_barrier((kv_next, *beside))
        if k == 1:
            q_keep, q_near = beside
        kv_steps.append(kv_next)
        if k % 2:
            groups.append(
                call(pair_kernel, "pair", shape(4, tok + 16, 2 * HEAD_SIZE), kv_steps[-2:])
            )
            kv_far.append([other_block(groups[-1], m) for m in range(1, n_blk)])
    capacity = max(2, 9 * tok * top_count // (8 * experts_all))
    pack = 8 // math.gcd(capacity, 8)
    slots, part_width = capacity * pack, model_width // pack
    targets = 2 * n_blk
    half_rows = n_blk * capacity
    *ranks, unpack, repack = call(
        functools.partial(slots_kernel, top_count, capacity, pack, n_blk, n_uly),
        "slots",
        [shape(targets, 1, tok, dtype=jnp.int32)] * chips
        + [shape(pack, half_rows, n_blk * slots), shape(pack, n_blk * slots, half_rows)],
        kv_steps,
        scalars=[where],
        vmem_mib=3 + pack * pack // 2,
    )
    scalars = [where, prefix_ids]
    pieces = [(k, 0) for k in range(0, chips, 2)]
    state = attend(
        groups, pieces, order, n_blk, scalars, q_keep, q_near, kv_steps[0], None, False
    )
    *ranks, unpack, repack, a, b, c, x, y, z = lax.optimization_barrier(
        [*ranks, unpack, repack, *state, w_gate, w_up, w_down]
    )
    (x, y, z), *kv_far = tied([x, y, z], *kv_far)
    mine, near = [x, y, z], [other_core(w) for w in (x, y, z)]
    pieces = [(k, m) for k in range(0, chips, 2) for m in range(1, n_blk)]
    attended, for_near = attend(
        [kv for group in kv_far for kv in group],
        pieces,
        order,
        n_blk,
        scalars,
        q_keep,
        q_near,
        kv_steps[0],
        [a, b, c],
        True,
    )
    blocks = max(1, model_width // 512)
    mixed, normed = call(
        project_kernel,
        "project",
        [shape(tok, model_width, dtype=F32), shape(tok, model_width)],
        [attended, other_core(for_near), hidden_in, post_gain[None, :]],
        scalars=[core_here],
        unused=[o_weight],
        scratch=[
            pltpu.VMEM((blocks, o_weight.shape[0], model_width // blocks), BF16),
            pltpu.SemaphoreType.DMA((blocks,)),
        ],
        vmem_mib=12,
        flops=4_000_000_000,
    )

    halves = shape(2, slots, part_width)

    def pick(k, rows):
        kernel = functools.partial(pick_kernel, capacity, pack)
        return call(kernel, "pick", [halves] * n_blk, [rows, ranks[k]])

    def expert(inbox):
        return call(
            functools.partial(expert_kernel, n_blk, pack),
            "expert",
            [halves] * n_blk,
            [*inbox, *experts, unpack, repack],
            scratch=[
                pltpu.VMEM((2, n_blk * slots, part_width), BF16),
                pltpu.VMEM((2, half_rows, model_width), BF16),
                pltpu.VMEM((2, half_rows, w_gate.shape[2]), BF16),
                pltpu.VMEM((2, pack, half_rows, part_width), BF16),
            ],
            vmem_mib=6 + pack,
        )

    def spread(k, back, adds):
        return call(
            functools.partial(spread_kernel, n_blk, pack, len(adds)),
            "spread",
            shape(tok, model_width),
            [*back, weights[k], *adds],
            scratch=[pltpu.VMEM((targets * slots, part_width), BF16)],
            vmem_mib=2 + pack,
        )

    def exchange(parts):
        return [other_block(x, m) if m else x for m, x in enumerate(parts)]

    way_back = [*range(1, chips), 0]
    normed, *experts = lax.optimization_barrier([normed, *mine, *near])
    rows = {0: normed}
    arrived, answers, back, total, weights = {}, {}, {}, {}, {}
    for now in range(2 * chips):
        new = {}
        if now + 1 < chips:
            new["rows", now + 1] = [next_chip(rows[now])]
        if now < chips:
            picked = pick(now, rows[now])
            new["arrived", now] = exchange(picked)
        if now >= chips:
            k = way_back[now - chips]
            new["back", k] = exchange(answers[k])
        if now > chips:
            k = way_back[now - chips - 1]
            before = [total[way_back[now - chips - 2]]] if now > chips + 1 else []
            new["total", k] = [next_chip(spread(k, back[k], before))]
        if chips - 1 <= now < 2 * chips - 1:
            k = way_back[now - chips + 1]
            new["answers", k] = expert(arrived[k])
        if chips <= now < 2 * chips:
            k = way_back[now - chips]
            new["weights", k] = [
                call(
                    functools.partial(weights_kernel, top_count, capacity, pack, n_blk, n_uly),
                    "weights",
                    shape(pack, 2 * tok, targets * slots),
                    [kv_steps[k]],
                    scalars=[where],
                    unused=[answers[k][0]],
                    vmem_mib=3 + pack * pack // 2,
                )
            ]
        flat = lax.optimization_barrier([x for group in new.values() for x in group])
        for (kind, k), group in new.items():
            group = [flat.pop(0) for _ in group]
            for name, table in (("arrived", arrived), ("answers", answers), ("back", back)):
                if kind == name:
                    table[k] = group
            for name, table in (("rows", rows), ("total", total), ("weights", weights)):
                if kind == name:
                    table[k] = group[0]
    before = [total[way_back[-2]]] if chips > 1 else []
    return spread(0, back[0], [*before, mixed])


def solution(mesh):
    rows = P(("blk", "uly"), None)
    in_specs = (
        rows,
        rows,
        rows,
        rows,
        P(("blk", "uly")),
        P(),
        P(),
        P(),
        rows,
        rows,
        P(("blk", "uly"), None, None),
        P(("blk", "uly"), None, None),
        P(("blk", "uly"), None, None),
    )
    return jax.shard_map(shards, mesh=mesh, in_specs=in_specs, out_specs=rows, check_vma=False)
```

```python
import functools
import math

import jax
import jax.numpy as jnp
from jax import lax
from jax.experimental import pallas as pl
from jax.experimental.pallas import tpu as pltpu
from jax.sharding import PartitionSpec as P

HEAD_SIZE = 128
FLOOR = -1e20
HIDDEN = -1e30
BF16, F32 = jnp.bfloat16, jnp.float32


def chip_ring(count):
    return list(range(0, 1)) + list(range(1, count, 2)) + list(range(2, count, 2))[::-1]


def call(
    kernel, name, out_shape, operands, scalars=(), scratch=(), unused=(), vmem_mib=4, flops=1000
):
    vmem = pl.BlockSpec(memory_space=pltpu.VMEM)
    several = isinstance(out_shape, (list, tuple))
    return pl.pallas_call(
        kernel,
        out_shape=out_shape,
        in_specs=[pl.BlockSpec(memory_space=pltpu.SMEM)] * len(scalars)
        + [vmem] * len(operands)
        + [pl.BlockSpec(memory_space=pl.ANY)] * len(unused),
        out_specs=[vmem] * len(out_shape) if several else vmem,
        scratch_shapes=list(scratch),
        compiler_params=pltpu.CompilerParams(vmem_limit_bytes=vmem_mib * 1024 * 1024),
        cost_estimate=pl.CostEstimate(flops=flops, bytes_accessed=1000, transcendentals=0),
        name=name,
    )(*scalars, *operands, *unused)


def message_kernel(core_ref, kv_ref, small_ref, keep, give):
    tok = kv_ref.shape[0]
    top_count = small_ref.shape[0] // 3
    first = core_ref[0] == 0
    k0, k1, v0, v1 = (kv_ref[:, i * HEAD_SIZE : (i + 1) * HEAD_SIZE] for i in range(4))
    v0, v1 = (v.astype(F32).T.astype(BF16) for v in (v0, v1))
    ids, gates, segs = (small_ref[i * top_count : (i + 1) * top_count] for i in range(3))
    share = gates / jnp.sum(gates, axis=0, keepdims=True)
    share_hi = share.astype(BF16).astype(F32)
    left = jnp.concatenate([ids, share_hi], axis=0)
    right = jnp.concatenate([share - share_hi, segs], axis=0)
    small = jnp.concatenate([left, right], axis=1).astype(BF16)
    keep[:tok, :HEAD_SIZE] = jnp.where(first, k0, k1)
    keep[:tok, HEAD_SIZE:] = jnp.where(first, v0, v1)
    keep[tok:, :] = small
    give[:tok, :HEAD_SIZE] = jnp.where(first, k1, k0)
    give[:tok, HEAD_SIZE:] = jnp.where(first, v1, v0)
    give[tok:, :] = small


def small_part(ref, j, tok):
    rows = ref[j, tok:, :].astype(F32)
    half = rows.shape[0] // 2
    return rows[:half, :tok], rows[half:, :tok], rows[:half, tok:], rows[half : half + 1, tok:]


def pair_kernel(a_ref, b_ref, out_ref):
    if len(a_ref.shape) < len(out_ref.shape):
        out_ref[0] = a_ref[...]
        out_ref[1] = b_ref[...]
    else:
        out_ref[: a_ref.shape[0]] = a_ref[...]
        out_ref[a_ref.shape[0] :] = b_ref[...]


def turn_kernel(core_ref, query_ref, keep, give):
    first = core_ref[0] == 0
    half = keep.shape[1]
    tok = query_ref.shape[0]
    for h in range(half // tok):
        a, b = (
            query_ref[:, g * (half // tok) * HEAD_SIZE + h * HEAD_SIZE :][:, :HEAD_SIZE]
            .astype(F32)
            .T.astype(BF16)
            for g in range(2)
        )
        keep[:, h * tok : (h + 1) * tok] = jnp.where(first, a, b)
        give[:, h * tok : (h + 1) * tok] = jnp.where(first, b, a)


def attend_kernel(
    pieces, order, n_blk, first, last, where_ref, prefix_ref, q_own, q_near, home_ref, *refs
):
    kv_refs, refs = refs[: len(pieces)], refs[len(pieces) :]
    if not first:
        top_in, sum_in, acc_in, *refs = refs
    if last:
        own_ref, near_ref, top_ref, sum_ref, acc_ref, *refs = refs
    else:
        top_ref, sum_ref, acc_ref, *refs = refs
    seg_ref, pre_ref, table, flags, flags_ref, sem, q_ref = refs
    columns, rows = q_own.shape[1], home_ref.shape[1] - 16
    each = kv_refs[0].shape[0]
    for tile in range(2 + each * len(pieces)):
        ref, at = (home_ref, tile) if tile < 2 else (kv_refs[(tile - 2) // each], (tile - 2) % each)
        seg_ref[tile] = small_part(ref, at, rows)[3]
        table[tile : tile + 1, :] = seg_ref[tile].astype(jnp.int32)
    low, high = table[:, :1], table[:, rows - 1 :]
    for g in range(2):
        segs = table[g : g + 1, :]
        prefix = jnp.zeros_like(segs)
        for s in range(prefix_ref.shape[0]):
            prefix = jnp.where(segs == s, prefix_ref[s], prefix)
        pre_ref[g] = prefix.astype(F32)
        found = jnp.maximum(
            jnp.where((segs >= low) & (segs <= high), 1, 0),
            jnp.where((prefix >= low) & (prefix <= high), 1, 0),
        )
        found = jnp.max(found.astype(F32), axis=1, keepdims=True)
        flags[g] = jnp.broadcast_to(found, table.shape).astype(jnp.int32)
    copy = pltpu.make_async_copy(flags, flags_ref, sem)
    copy.start()
    copy.wait()
    chips = len(order)
    scale = math.log2(math.e) / math.sqrt(HEAD_SIZE)
    width = 2 * rows
    q_ref[0] = q_own[...]
    q_ref[1] = q_near[...]
    if first:
        top_ref[...] = jnp.full_like(top_ref, FLOOR)
        sum_ref[...] = jnp.zeros_like(sum_ref)
        acc_ref[...] = jnp.zeros_like(acc_ref)
    else:
        top_ref[...] = top_in[...]
        sum_ref[...] = sum_in[...]
        acc_ref[...] = acc_in[...]
    blk, core, chip = where_ref[0], where_ref[1] % 2, where_ref[1] // 2
    place = sum(jnp.where(chip == z, i, 0) for i, z in enumerate(order))

    def start_of(k, m, j):
        at = lax.rem(place - k + chips, chips)
        chip_there = sum(jnp.where(at == i, z, 0) for i, z in enumerate(order))
        core_there = core + j - 2 * core * j
        return ((blk ^ m) * (2 * chips) + 2 * chip_there + core_there) * rows

    for number, (kv_ref, (k, m)) in enumerate(zip(kv_refs, pieces, strict=True)):

        def step(i, _, number=number, kv_ref=kv_ref, k=k, m=m):
            at, g = i // 2, i % 2
            tile = 2 + each * number + at
            key_start, query_start = start_of(k + at // 2, m, at % 2), start_of(0, 0, g)

            @pl.when((flags_ref[g, tile, 0] > 0) & (key_start <= query_start))
            def _():
                square = (rows, rows)
                key_pos = key_start + lax.broadcasted_iota(jnp.int32, square, 0)
                query_pos = query_start + lax.broadcasted_iota(jnp.int32, square, 1)
                key_seg = jnp.broadcast_to(seg_ref[tile], square).T
                visible = (key_pos <= query_pos) & (
                    (key_seg == seg_ref[g]) | (key_seg == pre_ref[g])
                )
                bias = jnp.where(visible, 0.0, HIDDEN)
                bias = jnp.concatenate([bias] * (width // rows), axis=1)
                key_tile = kv_ref[at, :rows, :HEAD_SIZE]
                value_tile = kv_ref[at, :rows, HEAD_SIZE:]
                for column in range(0, columns, width):
                    part = pl.ds(column, width)
                    scores = (
                        jnp.dot(key_tile, q_ref[g, :, part], preferred_element_type=F32) * scale
                        + bias
                    )
                    old_top = top_ref[g, :, part]
                    new_top = jnp.maximum(old_top, jnp.max(scores, axis=0, keepdims=True))
                    weights = jnp.exp2(scores - new_top)
                    rescale = jnp.exp2(old_top - new_top)
                    top_ref[g, :, part] = new_top
                    sum_ref[g, :, part] = sum_ref[g, :, part] * rescale + jnp.sum(
                        weights, axis=0, keepdims=True
                    )
                    acc_ref[g, :, part] = acc_ref[g, :, part] * rescale + jnp.dot(
                        value_tile, weights.astype(BF16), preferred_element_type=F32
                    )

            return 0

        lax.fori_loop(0, 2 * each, step, 0)
    if last:
        for g, out_ref in enumerate((own_ref, near_ref)):
            for h in range(columns // rows):
                part = pl.ds(h * rows, rows)
                result = acc_ref[g, :, part] / sum_ref[g, :, part]
                out_ref[:, h * HEAD_SIZE : (h + 1) * HEAD_SIZE] = result.T.astype(BF16)


def attend(kv_list, pieces, order, n_blk, scalars, q_own, q_near, home, state, last):
    head, columns = q_own.shape
    rows = home.shape[1] - 16
    tiles = 2 + kv_list[0].shape[0] * len(kv_list)
    first = not state
    state_shapes = [
        jax.ShapeDtypeStruct((2, 1, columns), F32),
        jax.ShapeDtypeStruct((2, 1, columns), F32),
        jax.ShapeDtypeStruct((2, head, columns), F32),
    ]
    scratch = [
        pltpu.VMEM((tiles, 1, rows), F32),
        pltpu.VMEM((2, 1, rows), F32),
        pltpu.VMEM((tiles, rows), jnp.int32),
        pltpu.VMEM((2, tiles, rows), jnp.int32),
        pltpu.SMEM((2, tiles, rows), jnp.int32),
        pltpu.SemaphoreType.DMA,
        pltpu.VMEM((2, head, columns), BF16),
    ]
    if last:
        out_shape = [jax.ShapeDtypeStruct((rows, columns // rows * head), BF16)] * 2
        scratch = [pltpu.VMEM(s.shape, s.dtype) for s in state_shapes] + scratch
    else:
        out_shape = state_shapes
    return call(
        functools.partial(attend_kernel, pieces, order, n_blk, first, last),
        "attend_last" if last else "attend_own",
        out_shape,
        [q_own, q_near, home, *kv_list, *(() if first else state)],
        scalars=scalars,
        scratch=scratch,
        vmem_mib=5 + len(kv_list) // 4,
        flops=8_000_000_000 if last else 1000,
    )


def project_kernel(
    core_ref, own_ref, got_ref, weight_ref, hidden_ref, gain_ref, mixed_ref, left_ref, right_ref
):
    core = core_ref[0]
    half = own_ref.shape[1]
    width = hidden_ref.shape[1]
    block = math.gcd(width, 512)
    own_at = pl.multiple_of(core * half, half)
    got_at = pl.multiple_of((1 - core) * half, half)
    total = jnp.zeros((own_ref.shape[0], 1), F32)
    for at in range(0, width, block):
        part = pl.ds(at, block)
        now = (
            hidden_ref[:, part].astype(F32)
            + jnp.dot(
                own_ref[...], weight_ref[pl.ds(own_at, half), part], preferred_element_type=F32
            )
            + jnp.dot(
                got_ref[...], weight_ref[pl.ds(got_at, half), part], preferred_element_type=F32
            )
        )
        mixed_ref[:, part] = now
        total = total + jnp.sum(now * now, axis=1, keepdims=True)
    factor = lax.rsqrt(total / width + 1e-06)
    side = width // 2
    for at, out_ref in ((0, left_ref), (side, right_ref)):
        part = pl.ds(at, side)
        out_ref[...] = (mixed_ref[:, part] * factor * gain_ref[:, part]).astype(BF16)


def sort_rows(kv_ref, where_ref, top_count, n_blk, n_uly):
    tok = kv_ref.shape[1] - 16
    blk, uly = where_ref[0], where_ref[1]
    ids, hi, lo, _ = (x[:top_count] for x in small_part(kv_ref, 0, tok))
    rows = [[], [], []]
    for target in range(2 * n_blk):
        m, j = target // 2, target % 2
        named = ids == ((blk ^ m) * n_uly + (uly ^ j)).astype(F32)
        for at, x in enumerate((jnp.ones_like(ids), hi, lo)):
            rows[at].append(jnp.sum(jnp.where(named, x, 0.0), axis=0, keepdims=True))
    hit, hi, lo = (jnp.concatenate(r, axis=0) for r in rows)
    earlier = lax.broadcasted_iota(jnp.int32, (tok, tok), 0)
    before = jnp.where(earlier < lax.broadcasted_iota(jnp.int32, (tok, tok), 1), 1.0, 0.0)
    rank = jnp.dot(hit.astype(BF16), before.astype(BF16), preferred_element_type=F32)
    return jnp.where(hit > 0.0, rank, -1e6), hi, lo


def weights_kernel(top_count, capacity, pack, n_blk, n_uly, where_ref, *refs):
    chips = (len(refs) - 1) // 2
    targets, slots = 2 * n_blk, capacity * pack
    for kv_ref, weight_ref in zip(refs[:chips], refs[-chips:], strict=True):
        tok = kv_ref.shape[1] - 16
        rank, hi, lo = sort_rows(kv_ref, where_ref, top_count, n_blk, n_uly)
        first = lax.broadcasted_iota(jnp.int32, rank.shape, 0).astype(F32) * slots
        spare = jnp.zeros((tok - 3 * targets, tok), F32)
        place = jnp.concatenate([rank + first, hi, lo, spare], axis=0).T
        for q in range(pack):
            for at in range(0, targets * slots, 128):
                width = min(128, targets * slots - at)
                lane = at + lax.broadcasted_iota(jnp.int32, (tok, width), 1).astype(F32)
                weight_hi = jnp.zeros(lane.shape, F32)
                weight_lo = jnp.zeros(lane.shape, F32)
                for t in range(at // slots, min(targets, -(-(at + width) // slots))):
                    hit = lane == place[:, t : t + 1] + q * capacity
                    weight_hi = jnp.where(hit, place[:, targets + t : targets + t + 1], weight_hi)
                    weight_lo = jnp.where(
                        hit, place[:, 2 * targets + t : 2 * targets + t + 1], weight_lo
                    )
                weight_ref[q, :tok, at : at + width] = weight_hi.astype(BF16)
                weight_ref[q, tok:, at : at + width] = weight_lo.astype(BF16)


def slots_kernel(top_count, capacity, pack, n_blk, n_uly, where_ref, *refs):
    chips = (len(refs) - 3) // 2
    unpack_ref, repack_ref = refs[-2:]
    targets = 2 * n_blk
    for kv_ref, rank_ref in zip(refs[:chips], refs[chips + 1 : -2], strict=True):
        rank = sort_rows(kv_ref, where_ref, top_count, n_blk, n_uly)[0].astype(jnp.int32)
        for target in range(targets):
            rank_ref[target] = rank[target : target + 1]
    for part in range(pack):
        for ref, row_axis in ((unpack_ref, 0), (repack_ref, 1)):
            row = lax.broadcasted_iota(jnp.int32, ref.shape[1:], row_axis)
            spot = lax.broadcasted_iota(jnp.int32, ref.shape[1:], 1 - row_axis)
            target = sum(jnp.where(row >= t * capacity, 1, 0) for t in range(1, n_blk))
            same = spot == row + target * (capacity * (pack - 1)) + part * capacity
            ref[part] = jnp.where(same, 1.0, 0.0).astype(BF16)


def pick_kernel(capacity, pack, left_ref, right_ref, rank_ref, *refs):
    targets, tok = rank_ref.shape[0], left_ref.shape[0]
    half = left_ref.shape[1]
    outs = refs[-(targets // 2) :]
    _, slots, width = outs[0].shape
    slot = lax.broadcasted_iota(jnp.int32, (slots, tok), 0)
    chosen = jnp.concatenate(
        [
            jnp.concatenate(
                [jnp.where(rank_ref[t] + q * capacity == slot, 1.0, 0.0) for q in range(pack)], axis=1
            )
            for t in range(targets)
        ],
        axis=0,
    ).astype(BF16)
    block = math.gcd(width, 512)
    for at in range(0, width, block):
        parts = jnp.concatenate(
            [
                (left_ref, right_ref)[(q * width + at) // half][
                    :, (q * width + at) % half : (q * width + at) % half + block
                ]
                for q in range(pack)
            ],
            axis=0,
        )
        rows = jnp.dot(chosen, parts, preferred_element_type=F32)
        for t in range(targets):
            outs[t // 2][t % 2, :, at : at + block] = rows[t * slots : (t + 1) * slots].astype(BF16)


def expert_kernel(n_blk, pack, *refs):
    ins, experts, (unpack_ref, repack_ref), refs = (
        refs[:n_blk],
        (refs[n_blk : n_blk + 3], refs[n_blk + 3 : n_blk + 6]),
        refs[n_blk + 6 : n_blk + 8],
        refs[n_blk + 8 :],
    )
    outs, (mail_ref, rows_ref, act_ref, answer_ref) = refs[-n_blk - 4 : -4], refs[-4:]
    _, slots, part_width = ins[0].shape
    block = math.gcd(part_width, 512)
    for j, (gate_ref, up_ref, down_ref) in enumerate(experts):
        mail_ref[j] = jnp.concatenate([r[j].astype(F32) for r in ins], axis=0).astype(BF16)
        for q in range(pack):
            for at in range(0, part_width, block):
                rows_ref[j, :, q * part_width + at : q * part_width + at + block] = jnp.dot(
                    unpack_ref[q], mail_ref[j, :, at : at + block], preferred_element_type=F32
                ).astype(BF16)
        inner = down_ref.shape[1]
        inner_block = math.gcd(inner, 256)

        def hidden(i, _, j=j, gate_ref=gate_ref, up_ref=up_ref):
            part = pl.ds(pl.multiple_of(i * inner_block, inner_block), inner_block)
            gate = jnp.dot(rows_ref[j], gate_ref[0, :, part], preferred_element_type=F32)
            up = jnp.dot(rows_ref[j], up_ref[0, :, part], preferred_element_type=F32)
            act_ref[j, :, part] = (gate / (1.0 + jnp.exp(-gate)) * up).astype(BF16)
            return 0

        lax.fori_loop(0, inner // inner_block, hidden, 0)
        for q in range(pack):

            def answer(i, _, j=j, q=q, down_ref=down_ref):
                at = i * block
                to = pl.ds(pl.multiple_of(at, block), block)
                part = pl.ds(pl.multiple_of(q * part_width + at, block), block)
                answer_ref[j, q, :, to] = jnp.dot(
                    act_ref[j], down_ref[0, :, part], preferred_element_type=F32
                ).astype(BF16)
                return 0

            lax.fori_loop(0, part_width // block, answer, 0)
        for at in range(0, part_width, block):
            mail = sum(
                jnp.dot(
                    repack_ref[q],
                    answer_ref[j, q, :, at : at + block],
                    preferred_element_type=F32,
                )
                for q in range(pack)
            )
            for m in range(n_blk):
                outs[m][j, :, at : at + block] = mail[m * slots : (m + 1) * slots].astype(BF16)


def spread_kernel(n_blk, pack, added, *refs):
    backs, weight_ref, adds = refs[:n_blk], refs[n_blk], refs[n_blk + 1 : n_blk + 1 + added]
    *outs, mail_ref = refs[n_blk + 1 + added :]
    _, slots, part_width = backs[0].shape
    tok, full = outs[0].shape[0], pack * part_width
    mails = [r[j].astype(F32) for r in backs for j in range(2)]
    mail_ref[...] = jnp.concatenate(mails, axis=0).astype(BF16)
    block = math.gcd(part_width, 512)

    def columns(arrays, at):
        side = full // len(arrays)
        return arrays[at // side].at[:, at % side : at % side + block]

    whole = [[r] for r in adds if r.shape[1] == full]
    halves = [r for r in adds if r.shape[1] < full]
    for q in range(pack):
        for at in range(0, part_width, block):
            both = jnp.dot(weight_ref[q], mail_ref[:, at : at + block], preferred_element_type=F32)
            to = q * part_width + at
            sums = both[:tok] + both[tok:]
            for arrays in whole + ([halves] if halves else []):
                sums = sums + columns(arrays, to)[...].astype(F32)
            columns(outs, to)[...] = sums.astype(BF16)


def shards(
    hidden_in,
    queries,
    keys,
    values,
    segment_ids,
    prefix_ids,
    o_weight,
    post_gain,
    expert_ids,
    gates,
    w_gate,
    w_up,
    w_down,
):
    tok, model_width = hidden_in.shape
    n_blk, n_uly = lax.axis_size("blk"), lax.axis_size("uly")
    chips = n_uly // 2
    experts_all = n_blk * n_uly
    top_count = expert_ids.shape[1]
    columns = queries.shape[1] // HEAD_SIZE // 2 * tok
    blk, uly = lax.axis_index("blk"), lax.axis_index("uly")
    core, chip = uly % 2, uly // 2
    me = blk * n_uly + uly
    core_here = core.astype(jnp.int32)[None]

    order = chip_ring(chips)
    ring_pairs = [
        (2 * order[i] + c, 2 * order[(i + 1) % chips] + c) for i in range(chips) for c in range(2)
    ]
    swap_pairs = [(u, u ^ 1) for u in range(n_uly)]
    next_chip = functools.partial(lax.ppermute, axis_name="uly", perm=ring_pairs)
    other_core = functools.partial(lax.ppermute, axis_name="uly", perm=swap_pairs)

    def other_block(x, m):
        return lax.ppermute(x, "blk", [(b, b ^ m) for b in range(n_blk)])

    def tied(*groups):
        flat = list(lax.optimization_barrier(tuple(x for group in groups for x in group)))
        return [[flat.pop(0) for _ in group] for group in groups]

    def shape(*dims, dtype=BF16):
        return jax.ShapeDtypeStruct(dims, dtype)

    keep, give = call(
        message_kernel,
        "message",
        [shape(tok + 16, 2 * HEAD_SIZE)] * 2,
        [
            jnp.concatenate([keys, values], axis=1),
            jnp.concatenate(
                [
                    expert_ids.T.astype(F32),
                    gates.T,
                    jnp.broadcast_to(segment_ids.astype(F32), (top_count, tok)),
                ]
            ),
        ],
        scalars=[core_here],
    )
    where = jnp.stack([blk, uly]).astype(jnp.int32)
    [keep, give], [where] = tied([keep, give], [where])
    kv_steps = [
        call(pair_kernel, "pair", shape(2, tok + 16, 2 * HEAD_SIZE), [keep, other_core(give)])
    ]
    [queries], _ = tied([queries], [kv_steps[0]])
    q_keep, q_give = call(
        turn_kernel, "turn", [shape(HEAD_SIZE, columns)] * 2, [queries], scalars=[core_here]
    )
    scalars = [where, prefix_ids]

    def attend_some(pieces, state, last):
        refs = [kv_far[k][m - 1] if m else kv_steps[k] for k, m in pieces]
        return attend(
            refs, pieces, order, n_blk, scalars, q_keep, q_near, kv_steps[0], state, last
        )

    kv_far, mine, near, state = [], [w_gate, w_up, w_down], [], None
    for k in range(chips):
        far = [other_block(kv_steps[k], m) for m in range(1, n_blk)]
        kv_next = [next_chip(kv_steps[k])] if k < chips - 1 else []
        beside = [q_keep, other_core(q_give)] if k == 0 else []
        if k >= chips - 2:
            here = mine[:1] if k == chips - 2 else mine[len(near) :]
            here, _ = tied(here, [kv_steps[k]])
            beside = beside + [other_core(w) for w in here]
        if k > 0:
            own = [(0, 0), (1, 0)] if k == 1 else [(k, 0)]
            state = attend_some([*own, *((k - 1, m) for m in range(1, n_blk))], state, False)
        kv_next, far, beside, state = tied(kv_next, far, beside, state or [])
        kv_steps += kv_next
        kv_far.append(far)
        if k == 0:
            q_keep, q_near = beside[:2]
        if k >= chips - 2:
            near += beside[2:] if k == 0 else beside
    last_pieces = [(chips - 1, m) for m in range(1, n_blk)]
    attended, for_near = attend_some(last_pieces, state, True)
    capacity = max(2, 9 * tok * top_count // (8 * experts_all))
    pack = 8 // math.gcd(capacity, 8)
    slots, part_width = capacity * pack, model_width // pack
    targets = 2 * n_blk
    half_rows = n_blk * capacity
    *ranks, unpack, repack = call(
        functools.partial(slots_kernel, top_count, capacity, pack, n_blk, n_uly),
        "slots",
        [shape(targets, 1, tok, dtype=jnp.int32)] * chips
        + [shape(pack, half_rows, n_blk * slots), shape(pack, n_blk * slots, half_rows)],
        kv_steps,
        scalars=[where],
        unused=[for_near],
        vmem_mib=3 + pack * pack // 2,
    )
    mixed, *normed = call(
        project_kernel,
        "project",
        [shape(tok, model_width, dtype=F32)] + [shape(tok, model_width // 2)] * 2,
        [attended, other_core(for_near), o_weight, hidden_in, post_gain[None, :]],
        scalars=[core_here],
    )

    halves = shape(2, slots, part_width)

    def pick(k, rows):
        kernel = functools.partial(pick_kernel, capacity, pack)
        return call(kernel, "pick", [halves] * n_blk, [*rows, ranks[k]])

    def expert(inbox):
        return call(
            functools.partial(expert_kernel, n_blk, pack),
            "expert",
            [halves] * n_blk,
            [*inbox, *experts, unpack, repack],
            scratch=[
                pltpu.VMEM((2, n_blk * slots, part_width), BF16),
                pltpu.VMEM((2, half_rows, model_width), BF16),
                pltpu.VMEM((2, half_rows, w_gate.shape[2]), BF16),
                pltpu.VMEM((2, pack, half_rows, part_width), BF16),
            ],
            vmem_mib=6 + pack,
        )

    def spread(k, back, adds, last):
        return call(
            functools.partial(spread_kernel, n_blk, pack, len(adds)),
            "spread",
            shape(tok, model_width) if last else [shape(tok, model_width // 2)] * 2,
            [*back, *weights[k], *adds],
            scratch=[pltpu.VMEM((targets * slots, part_width), BF16)],
            vmem_mib=2 + pack,
        )

    def exchange(parts):
        return [other_block(x, m) if m else x for m, x in enumerate(parts)]

    way_back = [*range(1, chips), 0]
    normed, experts = tied(normed, [*mine, *near])
    rows = {0: normed}
    arrived, answers, back, total, weights = {}, {}, {}, {}, {}
    tables = dict(
        rows=rows, arrived=arrived, answers=answers, back=back, total=total, weights=weights
    )
    for now in range(2 * chips):
        new = {}
        if now + 1 < chips:
            new["rows", now + 1] = [next_chip(x) for x in rows[now]]
        if now < chips:
            picked = pick(now, rows[now])
            new["arrived", now] = exchange(picked)
        if now >= chips:
            k = way_back[now - chips]
            new["back", k] = exchange(answers[k])
        if now > chips:
            k = way_back[now - chips - 1]
            before = total[way_back[now - chips - 2]] if now > chips + 1 else []
            new["total", k] = [next_chip(x) for x in spread(k, back[k], before, False)]
        if 1 <= now <= chips:
            new["answers", now - 1] = expert(arrived[now - 1])
        if 0 <= now - 1 - chips // 2 < chips:
            k = way_back[now - 1 - chips // 2]
            new["weights", k] = [
                call(
                    functools.partial(weights_kernel, top_count, capacity, pack, n_blk, n_uly),
                    "weights",
                    shape(pack, 2 * tok, targets * slots),
                    [kv_steps[k]],
                    scalars=[where],
                    unused=[arrived[min(now, chips) - 1][0]],
                    vmem_mib=3 + pack * pack // 2,
                )
            ]
        flat = lax.optimization_barrier([x for group in new.values() for x in group])
        for (kind, k), group in new.items():
            group = [flat.pop(0) for _ in group]
            tables[kind][k] = group
    before = total[way_back[-2]] if chips > 1 else []
    return spread(0, back[0], [*before, mixed], True)


def solution(mesh):
    rows = P(("blk", "uly"), None)
    in_specs = (
        rows,
        rows,
        rows,
        rows,
        P(("blk", "uly")),
        P(),
        P(),
        P(),
        rows,
        rows,
        P(("blk", "uly"), None, None),
        P(("blk", "uly"), None, None),
        P(("blk", "uly"), None, None),
    )
    return jax.shard_map(shards, mesh=mesh, in_specs=in_specs, out_specs=rows, check_vma=False)
```

```python
import functools
import math

import jax
import jax.numpy as jnp
from jax import lax
from jax.experimental import pallas as pl
from jax.experimental.pallas import tpu as pltpu
from jax.sharding import PartitionSpec as P

HEAD_SIZE = 128
FLOOR = -1e20
HIDDEN = -1e30
BF16, F32 = jnp.bfloat16, jnp.float32


def chip_ring(count):
    return list(range(0, 1)) + list(range(1, count, 2)) + list(range(2, count, 2))[::-1]


def call(
    kernel, name, out_shape, operands, scalars=(), scratch=(), unused=(), vmem_mib=4, flops=1000
):
    vmem = pl.BlockSpec(memory_space=pltpu.VMEM)
    several = isinstance(out_shape, (list, tuple))
    return pl.pallas_call(
        kernel,
        out_shape=out_shape,
        in_specs=[pl.BlockSpec(memory_space=pltpu.SMEM)] * len(scalars)
        + [vmem] * len(operands)
        + [pl.BlockSpec(memory_space=pl.ANY)] * len(unused),
        out_specs=[vmem] * len(out_shape) if several else vmem,
        scratch_shapes=list(scratch),
        compiler_params=pltpu.CompilerParams(vmem_limit_bytes=vmem_mib * 1024 * 1024),
        cost_estimate=pl.CostEstimate(flops=flops, bytes_accessed=1000, transcendentals=0),
        name=name,
    )(*scalars, *operands, *unused)


def message_kernel(core_ref, kv_ref, small_ref, gates_ref, keep, give):
    tok = kv_ref.shape[0]
    top_count = gates_ref.shape[0]
    first = core_ref[0] == 0
    k0, k1, v0, v1 = (kv_ref[:, i * HEAD_SIZE : (i + 1) * HEAD_SIZE] for i in range(4))
    v0, v1 = (v.astype(F32).T.astype(BF16) for v in (v0, v1))
    ids, segs = (small_ref[i * top_count : (i + 1) * top_count].astype(F32) for i in range(2))
    gates = gates_ref[...]
    share = gates / jnp.sum(gates, axis=0, keepdims=True)
    share_hi = share.astype(BF16).astype(F32)
    left = jnp.concatenate([ids, share_hi], axis=0)
    right = jnp.concatenate([share - share_hi, segs], axis=0)
    small = jnp.concatenate([left, right], axis=1).astype(BF16)
    keep[:tok, :HEAD_SIZE] = jnp.where(first, k0, k1)
    keep[:tok, HEAD_SIZE:] = jnp.where(first, v0, v1)
    keep[tok:, :] = small
    give[:tok, :HEAD_SIZE] = jnp.where(first, k1, k0)
    give[:tok, HEAD_SIZE:] = jnp.where(first, v1, v0)
    give[tok:, :] = small


def small_part(ref, j, tok):
    rows = ref[j, tok:, :].astype(F32)
    half = rows.shape[0] // 2
    return rows[:half, :tok], rows[half:, :tok], rows[:half, tok:], rows[half : half + 1, tok:]


def pair_kernel(a_ref, b_ref, out_ref):
    if len(a_ref.shape) < len(out_ref.shape):
        out_ref[0] = a_ref[...]
        out_ref[1] = b_ref[...]
    else:
        out_ref[: a_ref.shape[0]] = a_ref[...]
        out_ref[a_ref.shape[0] :] = b_ref[...]


def turn_kernel(core_ref, query_ref, keep, give):
    first = core_ref[0] == 0
    half = keep.shape[1]
    tok = query_ref.shape[0]
    for h in range(half // tok):
        a, b = (
            query_ref[:, g * (half // tok) * HEAD_SIZE + h * HEAD_SIZE :][:, :HEAD_SIZE]
            .astype(F32)
            .T.astype(BF16)
            for g in range(2)
        )
        keep[:, h * tok : (h + 1) * tok] = jnp.where(first, a, b)
        give[:, h * tok : (h + 1) * tok] = jnp.where(first, b, a)


def attend_kernel(
    pieces, order, n_blk, first, last, where_ref, prefix_ref, q_own, q_near, home_ref, *refs
):
    kv_refs, refs = refs[: len(pieces)], refs[len(pieces) :]
    if not first:
        top_in, sum_in, acc_in, *refs = refs
    if last:
        own_ref, near_ref, top_ref, sum_ref, acc_ref, *refs = refs
    else:
        top_ref, sum_ref, acc_ref, *refs = refs
    seg_ref, pre_ref, table, flags, flags_ref, sem, q_ref = refs
    columns, rows = q_own.shape[1], home_ref.shape[1] - 16
    each = kv_refs[0].shape[0]
    for tile in range(2 + each * len(pieces)):
        ref, at = (home_ref, tile) if tile < 2 else (kv_refs[(tile - 2) // each], (tile - 2) % each)
        seg_ref[tile] = small_part(ref, at, rows)[3]
        table[tile : tile + 1, :] = seg_ref[tile].astype(jnp.int32)
    low, high = table[:, :1], table[:, rows - 1 :]
    for g in range(2):
        segs = table[g : g + 1, :]
        prefix = jnp.zeros_like(segs)
        for s in range(prefix_ref.shape[0]):
            prefix = jnp.where(segs == s, prefix_ref[s], prefix)
        pre_ref[g] = prefix.astype(F32)
        found = jnp.maximum(
            jnp.where((segs >= low) & (segs <= high), 1, 0),
            jnp.where((prefix >= low) & (prefix <= high), 1, 0),
        )
        found = jnp.max(found.astype(F32), axis=1, keepdims=True)
        flags[g] = jnp.broadcast_to(found, table.shape).astype(jnp.int32)
    copy = pltpu.make_async_copy(flags, flags_ref, sem)
    copy.start()
    copy.wait()
    chips = len(order)
    scale = math.log2(math.e) / math.sqrt(HEAD_SIZE)
    width = 2 * rows
    q_ref[0] = q_own[...]
    q_ref[1] = q_near[...]
    if first:
        top_ref[...] = jnp.full_like(top_ref, FLOOR)
        sum_ref[...] = jnp.zeros_like(sum_ref)
        acc_ref[...] = jnp.zeros_like(acc_ref)
    else:
        top_ref[...] = top_in[...]
        sum_ref[...] = sum_in[...]
        acc_ref[...] = acc_in[...]
    blk, core, chip = where_ref[0], where_ref[1] % 2, where_ref[1] // 2
    place = sum(jnp.where(chip == z, i, 0) for i, z in enumerate(order))

    def start_of(k, m, j):
        at = lax.rem(place - k + chips, chips)
        chip_there = sum(jnp.where(at == i, z, 0) for i, z in enumerate(order))
        core_there = core + j - 2 * core * j
        return ((blk ^ m) * (2 * chips) + 2 * chip_there + core_there) * rows

    for number, (kv_ref, (k, m)) in enumerate(zip(kv_refs, pieces, strict=True)):

        def step(i, _, number=number, kv_ref=kv_ref, k=k, m=m):
            at, g = i // 2, i % 2
            tile = 2 + each * number + at
            key_start, query_start = start_of(k + at // 2, m, at % 2), start_of(0, 0, g)

            @pl.when((flags_ref[g, tile, 0] > 0) & (key_start <= query_start))
            def _():
                square = (rows, rows)
                key_pos = key_start + lax.broadcasted_iota(jnp.int32, square, 0)
                query_pos = query_start + lax.broadcasted_iota(jnp.int32, square, 1)
                key_seg = jnp.broadcast_to(seg_ref[tile], square).T
                visible = (key_pos <= query_pos) & (
                    (key_seg == seg_ref[g]) | (key_seg == pre_ref[g])
                )
                bias = jnp.where(visible, 0.0, HIDDEN)
                bias = jnp.concatenate([bias] * (width // rows), axis=1)
                key_tile = kv_ref[at, :rows, :HEAD_SIZE]
                value_tile = kv_ref[at, :rows, HEAD_SIZE:]
                for column in range(0, columns, width):
                    part = pl.ds(column, width)
                    scores = (
                        jnp.dot(key_tile, q_ref[g, :, part], preferred_element_type=F32) * scale
                        + bias
                    )
                    old_top = top_ref[g, :, part]
                    new_top = jnp.maximum(old_top, jnp.max(scores, axis=0, keepdims=True))
                    weights = jnp.exp2(scores - new_top)
                    rescale = jnp.exp2(old_top - new_top)
                    top_ref[g, :, part] = new_top
                    sum_ref[g, :, part] = sum_ref[g, :, part] * rescale + jnp.sum(
                        weights, axis=0, keepdims=True
                    )
                    acc_ref[g, :, part] = acc_ref[g, :, part] * rescale + jnp.dot(
                        value_tile, weights.astype(BF16), preferred_element_type=F32
                    )

            return 0

        lax.fori_loop(0, 2 * each, step, 0)
    if last:
        for g, out_ref in enumerate((own_ref, near_ref)):
            for h in range(columns // rows):
                part = pl.ds(h * rows, rows)
                result = acc_ref[g, :, part] / sum_ref[g, :, part]
                out_ref[:, h * HEAD_SIZE : (h + 1) * HEAD_SIZE] = result.T.astype(BF16)


def attend(kv_list, pieces, order, n_blk, scalars, q_own, q_near, home, state, last):
    head, columns = q_own.shape
    rows = home.shape[1] - 16
    tiles = 2 + kv_list[0].shape[0] * len(kv_list)
    first = not state
    state_shapes = [
        jax.ShapeDtypeStruct((2, 1, columns), F32),
        jax.ShapeDtypeStruct((2, 1, columns), F32),
        jax.ShapeDtypeStruct((2, head, columns), F32),
    ]
    scratch = [
        pltpu.VMEM((tiles, 1, rows), F32),
        pltpu.VMEM((2, 1, rows), F32),
        pltpu.VMEM((tiles, rows), jnp.int32),
        pltpu.VMEM((2, tiles, rows), jnp.int32),
        pltpu.SMEM((2, tiles, rows), jnp.int32),
        pltpu.SemaphoreType.DMA,
        pltpu.VMEM((2, head, columns), BF16),
    ]
    if last:
        out_shape = [jax.ShapeDtypeStruct((rows, columns // rows * head), BF16)] * 2
        scratch = [pltpu.VMEM(s.shape, s.dtype) for s in state_shapes] + scratch
    else:
        out_shape = state_shapes
    return call(
        functools.partial(attend_kernel, pieces, order, n_blk, first, last),
        "attend_last" if last else "attend_own",
        out_shape,
        [q_own, q_near, home, *kv_list, *(() if first else state)],
        scalars=scalars,
        scratch=scratch,
        vmem_mib=5 + len(kv_list) // 4,
        flops=8_000_000_000 if last else 1000,
    )


def project_kernel(
    core_ref, own_ref, got_ref, weight_ref, hidden_ref, gain_ref, mixed_ref, left_ref, right_ref
):
    core = core_ref[0]
    half = own_ref.shape[1]
    width = hidden_ref.shape[1]
    block = math.gcd(width, 512)
    own_at = pl.multiple_of(core * half, half)
    got_at = pl.multiple_of((1 - core) * half, half)
    total = jnp.zeros((own_ref.shape[0], 1), F32)
    for at in range(0, width, block):
        part = pl.ds(at, block)
        now = (
            hidden_ref[:, part].astype(F32)
            + jnp.dot(
                own_ref[...], weight_ref[pl.ds(own_at, half), part], preferred_element_type=F32
            )
            + jnp.dot(
                got_ref[...], weight_ref[pl.ds(got_at, half), part], preferred_element_type=F32
            )
        )
        mixed_ref[:, part] = now
        total = total + jnp.sum(now * now, axis=1, keepdims=True)
    factor = lax.rsqrt(total / width + 1e-06)
    side = width // 2
    for at, out_ref in ((0, left_ref), (side, right_ref)):
        part = pl.ds(at, side)
        out_ref[...] = (mixed_ref[:, part] * factor * gain_ref[:, part]).astype(BF16)


def sort_rows(kv_ref, where_ref, top_count, n_blk, n_uly):
    tok = kv_ref.shape[1] - 16
    blk, uly = where_ref[0], where_ref[1]
    ids, hi, lo, _ = (x[:top_count] for x in small_part(kv_ref, 0, tok))
    rows = [[], [], []]
    for target in range(2 * n_blk):
        m, j = target // 2, target % 2
        named = ids == ((blk ^ m) * n_uly + (uly ^ j)).astype(F32)
        for at, x in enumerate((jnp.ones_like(ids), hi, lo)):
            rows[at].append(jnp.sum(jnp.where(named, x, 0.0), axis=0, keepdims=True))
    hit, hi, lo = (jnp.concatenate(r, axis=0) for r in rows)
    earlier = lax.broadcasted_iota(jnp.int32, (tok, tok), 0)
    before = jnp.where(earlier < lax.broadcasted_iota(jnp.int32, (tok, tok), 1), 1.0, 0.0)
    rank = jnp.dot(hit.astype(BF16), before.astype(BF16), preferred_element_type=F32)
    return jnp.where(hit > 0.0, rank, -1e6), hi, lo


def weights_kernel(top_count, capacity, pack, n_blk, n_uly, where_ref, *refs):
    chips = (len(refs) - 1) // 2
    targets, slots = 2 * n_blk, capacity * pack
    for kv_ref, weight_ref in zip(refs[:chips], refs[-chips:], strict=True):
        tok = kv_ref.shape[1] - 16
        rank, hi, lo = sort_rows(kv_ref, where_ref, top_count, n_blk, n_uly)
        first = lax.broadcasted_iota(jnp.int32, rank.shape, 0).astype(F32) * slots
        spare = jnp.zeros((tok - 3 * targets, tok), F32)
        place = jnp.concatenate([rank + first, hi, lo, spare], axis=0).T
        for q in range(pack):
            for at in range(0, targets * slots, 128):
                width = min(128, targets * slots - at)
                lane = at + lax.broadcasted_iota(jnp.int32, (tok, width), 1).astype(F32)
                weight_hi = jnp.zeros(lane.shape, F32)
                weight_lo = jnp.zeros(lane.shape, F32)
                for t in range(at // slots, min(targets, -(-(at + width) // slots))):
                    hit = lane == place[:, t : t + 1] + q * capacity
                    weight_hi = jnp.where(hit, place[:, targets + t : targets + t + 1], weight_hi)
                    weight_lo = jnp.where(
                        hit, place[:, 2 * targets + t : 2 * targets + t + 1], weight_lo
                    )
                weight_ref[q, :tok, at : at + width] = weight_hi.astype(BF16)
                weight_ref[q, tok:, at : at + width] = weight_lo.astype(BF16)


def slots_kernel(top_count, capacity, pack, n_blk, n_uly, where_ref, *refs):
    chips = (len(refs) - 3) // 2
    unpack_ref, repack_ref = refs[-2:]
    targets = 2 * n_blk
    for kv_ref, rank_ref in zip(refs[:chips], refs[chips + 1 : -2], strict=True):
        rank = sort_rows(kv_ref, where_ref, top_count, n_blk, n_uly)[0].astype(jnp.int32)
        for target in range(targets):
            rank_ref[target] = rank[target : target + 1]
    for part in range(pack):
        for ref, row_axis in ((unpack_ref, 0), (repack_ref, 1)):
            row = lax.broadcasted_iota(jnp.int32, ref.shape[1:], row_axis)
            spot = lax.broadcasted_iota(jnp.int32, ref.shape[1:], 1 - row_axis)
            target = sum(jnp.where(row >= t * capacity, 1, 0) for t in range(1, n_blk))
            same = spot == row + target * (capacity * (pack - 1)) + part * capacity
            ref[part] = jnp.where(same, 1.0, 0.0).astype(BF16)


def pick_kernel(capacity, pack, left_ref, right_ref, rank_ref, *refs):
    targets, tok = rank_ref.shape[0], left_ref.shape[0]
    half = left_ref.shape[1]
    outs = refs[-(targets // 2) :]
    _, slots, width = outs[0].shape
    slot = lax.broadcasted_iota(jnp.int32, (slots, tok), 0)
    chosen = jnp.concatenate(
        [
            jnp.concatenate(
                [jnp.where(rank_ref[t] + q * capacity == slot, 1.0, 0.0) for q in range(pack)], axis=1
            )
            for t in range(targets)
        ],
        axis=0,
    ).astype(BF16)
    block = math.gcd(width, 512)
    for at in range(0, width, block):
        parts = jnp.concatenate(
            [
                (left_ref, right_ref)[(q * width + at) // half][
                    :, (q * width + at) % half : (q * width + at) % half + block
                ]
                for q in range(pack)
            ],
            axis=0,
        )
        rows = jnp.dot(chosen, parts, preferred_element_type=F32)
        for t in range(targets):
            outs[t // 2][t % 2, :, at : at + block] = rows[t * slots : (t + 1) * slots].astype(BF16)


def expert_kernel(n_blk, pack, *refs):
    ins, experts, (unpack_ref, repack_ref), refs = (
        refs[:n_blk],
        (refs[n_blk : n_blk + 3], refs[n_blk + 3 : n_blk + 6]),
        refs[n_blk + 6 : n_blk + 8],
        refs[n_blk + 8 :],
    )
    outs, (mail_ref, rows_ref, act_ref, answer_ref) = refs[-n_blk - 4 : -4], refs[-4:]
    _, slots, part_width = ins[0].shape
    block = math.gcd(part_width, 512)
    for j, (gate_ref, up_ref, down_ref) in enumerate(experts):
        mail_ref[j] = jnp.concatenate([r[j].astype(F32) for r in ins], axis=0).astype(BF16)
        for q in range(pack):
            for at in range(0, part_width, block):
                rows_ref[j, :, q * part_width + at : q * part_width + at + block] = jnp.dot(
                    unpack_ref[q], mail_ref[j, :, at : at + block], preferred_element_type=F32
                ).astype(BF16)
        inner = down_ref.shape[1]
        inner_block = math.gcd(inner, 256)

        def hidden(i, _, j=j, gate_ref=gate_ref, up_ref=up_ref):
            part = pl.ds(pl.multiple_of(i * inner_block, inner_block), inner_block)
            gate = jnp.dot(rows_ref[j], gate_ref[0, :, part], preferred_element_type=F32)
            up = jnp.dot(rows_ref[j], up_ref[0, :, part], preferred_element_type=F32)
            act_ref[j, :, part] = (gate / (1.0 + jnp.exp(-gate)) * up).astype(BF16)
            return 0

        lax.fori_loop(0, inner // inner_block, hidden, 0)
        for q in range(pack):

            def answer(i, _, j=j, q=q, down_ref=down_ref):
                at = i * block
                to = pl.ds(pl.multiple_of(at, block), block)
                part = pl.ds(pl.multiple_of(q * part_width + at, block), block)
                answer_ref[j, q, :, to] = jnp.dot(
                    act_ref[j], down_ref[0, :, part], preferred_element_type=F32
                ).astype(BF16)
                return 0

            lax.fori_loop(0, part_width // block, answer, 0)
        for at in range(0, part_width, block):
            mail = sum(
                jnp.dot(
                    repack_ref[q],
                    answer_ref[j, q, :, at : at + block],
                    preferred_element_type=F32,
                )
                for q in range(pack)
            )
            for m in range(n_blk):
                outs[m][j, :, at : at + block] = mail[m * slots : (m + 1) * slots].astype(BF16)


def spread_kernel(n_blk, pack, added, *refs):
    backs, weight_ref, adds = refs[:n_blk], refs[n_blk], refs[n_blk + 1 : n_blk + 1 + added]
    *outs, mail_ref = refs[n_blk + 1 + added :]
    _, slots, part_width = backs[0].shape
    tok, full = outs[0].shape[0], pack * part_width
    mails = [r[j].astype(F32) for r in backs for j in range(2)]
    mail_ref[...] = jnp.concatenate(mails, axis=0).astype(BF16)
    block = math.gcd(part_width, 512)

    def columns(arrays, at):
        side = full // len(arrays)
        return arrays[at // side].at[:, at % side : at % side + block]

    whole = [[r] for r in adds if r.shape[1] == full]
    halves = [r for r in adds if r.shape[1] < full]
    for q in range(pack):
        for at in range(0, part_width, block):
            both = jnp.dot(weight_ref[q], mail_ref[:, at : at + block], preferred_element_type=F32)
            to = q * part_width + at
            sums = both[:tok] + both[tok:]
            for arrays in whole + ([halves] if halves else []):
                sums = sums + columns(arrays, to)[...].astype(F32)
            columns(outs, to)[...] = sums.astype(BF16)


def shards(
    hidden_in,
    queries,
    keys,
    values,
    segment_ids,
    prefix_ids,
    o_weight,
    post_gain,
    expert_ids,
    gates,
    w_gate,
    w_up,
    w_down,
):
    tok, model_width = hidden_in.shape
    n_blk, n_uly = lax.axis_size("blk"), lax.axis_size("uly")
    chips = n_uly // 2
    experts_all = n_blk * n_uly
    top_count = expert_ids.shape[1]
    columns = queries.shape[1] // HEAD_SIZE // 2 * tok
    blk, uly = lax.axis_index("blk"), lax.axis_index("uly")
    core, chip = uly % 2, uly // 2
    me = blk * n_uly + uly
    core_here = core.astype(jnp.int32)[None]

    order = chip_ring(chips)
    ring_pairs = [
        (2 * order[i] + c, 2 * order[(i + 1) % chips] + c) for i in range(chips) for c in range(2)
    ]
    swap_pairs = [(u, u ^ 1) for u in range(n_uly)]
    next_chip = functools.partial(lax.ppermute, axis_name="uly", perm=ring_pairs)
    other_core = functools.partial(lax.ppermute, axis_name="uly", perm=swap_pairs)

    def other_block(x, m):
        return lax.ppermute(x, "blk", [(b, b ^ m) for b in range(n_blk)])

    def tied(*groups):
        flat = list(lax.optimization_barrier(tuple(x for group in groups for x in group)))
        return [[flat.pop(0) for _ in group] for group in groups]

    def shape(*dims, dtype=BF16):
        return jax.ShapeDtypeStruct(dims, dtype)

    keep, give = call(
        message_kernel,
        "message",
        [shape(tok + 16, 2 * HEAD_SIZE)] * 2,
        [
            jnp.concatenate([keys, values], axis=1),
            jnp.concatenate([expert_ids.T, jnp.broadcast_to(segment_ids, (top_count, tok))]),
            gates.T,
        ],
        scalars=[core_here],
    )
    where = jnp.stack([blk, uly]).astype(jnp.int32)
    [keep, give], [where] = tied([keep, give], [where])
    kv_steps = [
        call(pair_kernel, "pair", shape(2, tok + 16, 2 * HEAD_SIZE), [keep, other_core(give)])
    ]
    [queries], _ = tied([queries], [kv_steps[0]])
    q_keep, q_give = call(
        turn_kernel, "turn", [shape(HEAD_SIZE, columns)] * 2, [queries], scalars=[core_here]
    )
    scalars = [where, prefix_ids]

    def attend_some(pieces, state, last):
        refs = [kv_far[k][m - 1] if m else kv_steps[k] for k, m in pieces]
        return attend(
            refs, pieces, order, n_blk, scalars, q_keep, q_near, kv_steps[0], state, last
        )

    kv_far, mine, near, state = [], [w_gate, w_up, w_down], [], None
    for k in range(chips):
        far = [other_block(kv_steps[k], m) for m in range(1, n_blk)]
        kv_next = [next_chip(kv_steps[k])] if k < chips - 1 else []
        beside = [q_keep, other_core(q_give)] if k == 0 else []
        if k >= chips - 2:
            here = mine[:1] if k == chips - 2 else mine[len(near) :]
            here, _ = tied(here, [kv_steps[k]])
            beside = beside + [other_core(w) for w in here]
        if k > 0:
            own = [(0, 0), (1, 0)] if k == 1 else [(k, 0)]
            state = attend_some([*own, *((k - 1, m) for m in range(1, n_blk))], state, False)
        kv_next, far, beside, state = tied(kv_next, far, beside, state or [])
        kv_steps += kv_next
        kv_far.append(far)
        if k == 0:
            q_keep, q_near = beside[:2]
        if k >= chips - 2:
            near += beside[2:] if k == 0 else beside
    last_pieces = [(chips - 1, m) for m in range(1, n_blk)]
    attended, for_near = attend_some(last_pieces, state, True)
    capacity = max(2, 9 * tok * top_count // (8 * experts_all))
    pack = 8 // math.gcd(capacity, 8)
    slots, part_width = capacity * pack, model_width // pack
    targets = 2 * n_blk
    half_rows = n_blk * capacity
    *ranks, unpack, repack = call(
        functools.partial(slots_kernel, top_count, capacity, pack, n_blk, n_uly),
        "slots",
        [shape(targets, 1, tok, dtype=jnp.int32)] * chips
        + [shape(pack, half_rows, n_blk * slots), shape(pack, n_blk * slots, half_rows)],
        kv_steps,
        scalars=[where],
        unused=[for_near],
        vmem_mib=3 + pack * pack // 2,
    )
    mixed, *normed = call(
        project_kernel,
        "project",
        [shape(tok, model_width, dtype=F32)] + [shape(tok, model_width // 2)] * 2,
        [attended, other_core(for_near), o_weight, hidden_in, post_gain[None, :]],
        scalars=[core_here],
    )

    halves = shape(2, slots, part_width)

    def pick(k, rows):
        kernel = functools.partial(pick_kernel, capacity, pack)
        return call(kernel, "pick", [halves] * n_blk, [*rows, ranks[k]])

    def expert(inbox):
        return call(
            functools.partial(expert_kernel, n_blk, pack),
            "expert",
            [halves] * n_blk,
            [*inbox, *experts, unpack, repack],
            scratch=[
                pltpu.VMEM((2, n_blk * slots, part_width), BF16),
                pltpu.VMEM((2, half_rows, model_width), BF16),
                pltpu.VMEM((2, half_rows, w_gate.shape[2]), BF16),
                pltpu.VMEM((2, pack, half_rows, part_width), BF16),
            ],
            vmem_mib=6 + pack,
        )

    def spread(k, back, adds, last):
        return call(
            functools.partial(spread_kernel, n_blk, pack, len(adds)),
            "spread",
            shape(tok, model_width) if last else [shape(tok, model_width // 2)] * 2,
            [*back, *weights[k], *adds],
            scratch=[pltpu.VMEM((targets * slots, part_width), BF16)],
            vmem_mib=2 + pack,
        )

    def exchange(parts):
        return [other_block(x, m) if m else x for m, x in enumerate(parts)]

    way_back = [*range(1, chips), 0]
    normed, experts = tied(normed, [*mine, *near])
    rows = {0: normed}
    arrived, answers, back, total, weights = {}, {}, {}, {}, {}
    tables = dict(
        rows=rows, arrived=arrived, answers=answers, back=back, total=total, weights=weights
    )
    for now in range(2 * chips):
        new = {}
        if now + 1 < chips:
            new["rows", now + 1] = [next_chip(x) for x in rows[now]]
        if now < chips:
            picked = pick(now, rows[now])
            new["arrived", now] = exchange(picked)
        if now >= chips:
            k = way_back[now - chips]
            new["back", k] = exchange(answers[k])
        if now > chips:
            k = way_back[now - chips - 1]
            before = total[way_back[now - chips - 2]] if now > chips + 1 else []
            new["total", k] = [next_chip(x) for x in spread(k, back[k], before, False)]
        if 1 <= now <= chips:
            new["answers", now - 1] = expert(arrived[now - 1])
        if 0 <= now - 1 - chips // 2 < chips:
            k = way_back[now - 1 - chips // 2]
            new["weights", k] = [
                call(
                    functools.partial(weights_kernel, top_count, capacity, pack, n_blk, n_uly),
                    "weights",
                    shape(pack, 2 * tok, targets * slots),
                    [kv_steps[k]],
                    scalars=[where],
                    unused=[arrived[min(now, chips) - 1][0]],
                    vmem_mib=3 + pack * pack // 2,
                )
            ]
        flat = lax.optimization_barrier([x for group in new.values() for x in group])
        for (kind, k), group in new.items():
            group = [flat.pop(0) for _ in group]
            tables[kind][k] = group
    before = total[way_back[-2]] if chips > 1 else []
    return spread(0, back[0], [*before, mixed], True)


def solution(mesh):
    rows = P(("blk", "uly"), None)
    in_specs = (
        rows,
        rows,
        rows,
        rows,
        P(("blk", "uly")),
        P(),
        P(),
        P(),
        rows,
        rows,
        P(("blk", "uly"), None, None),
        P(("blk", "uly"), None, None),
        P(("blk", "uly"), None, None),
    )
    return jax.shard_map(shards, mesh=mesh, in_specs=in_specs, out_specs=rows, check_vma=False)
```
